512 devices in a mesh: dom: 64 (over z, x), head: 8 (over y, core).
Axes of the slice: x: 4, y: 4, z: 16, core: 2. Of those that a mesh axis runs over, the one named last changes fastest.
Arguments:
- features: bfloat16 [262144, 768], P(('dom', 'head')), may hold values from -6.5 to 6.5
- qkv_weight: bfloat16 [768, 1536], replicated, may hold values from -0.21650635 to 0.21650635
- out_weight: bfloat16 [512, 768], replicated, may hold values from -0.25 to 0.25
- attn_gain: float32 [768], replicated, may hold values from 0.1 to 1.9
- up_weight: bfloat16 [768, 1536], P(None, 'dom'), may hold values from -0.21875 to 0.21875
- down_weight: bfloat16 [1536, 768], P('dom'), may hold values from -0.15625 to 0.15625
- final_gain: float32 [768], replicated, may hold values from 0.1 to 1.9
- node_order: int32 [262144], P('dom'), may hold values from 0 to 262143, as said below
- dest_part: int32 [2048, 2], P('dom'), may hold values from 0 to 63, all different within a row; in each aligned block of 32 rows (0 to 31, 32 to 63, ...) at most 2 rows name the same one
- key_block: int32 [2048, 2], P('dom'), may hold values from 0 to 31
- row_count: int32 [2048], P('dom'), may hold values from 16 to 128, as said below
Outputs:
- output: bfloat16 [262144, 768], P(('dom', 'head'))
The draws below stay inside these ranges and needn't reach their ends.
Inputs may be any that keep to these rules, and one draw needn't show every extreme that they name: The entries node_order[p * 4096] to node_order[(p + 1) * 4096 - 1] are the nodes p * 4096 to (p + 1) * 4096 - 1, each once. `dest_part`: the 2 entries of a row are different partitions. Among the 32 rows of one partition no partition is named more than 2 times, and one is named exactly 2 times in some partitions. `row_count`: some block has all 128 nodes valid.
All inputs are finite; a program needn't handle non-finite values.
Results may differ from the reference program's by a relative error of at most 0.014.
Values may be sent and summed in bfloat16 or wider, within the bound.
A program may use at most 128 MiB of HBM per device.

```python
import math
import jax
import jax.numpy as jnp
import numpy as np
from jax import lax

D = 768
HEADS = 8
HD = 64
FF = 1536
BLK = 128
TOP = 2
BLOCKS = 32
CAP = 2
NPART = 4096
NODES = 262144
N_DOM = 64


def draw_features(key, part):
    key = jax.random.fold_in(key, 11)
    base_key = jax.random.fold_in(key, 0)
    return jnp.clip(jax.random.normal(base_key, (NODES, D), jnp.float32), -6.0, 6.0).astype(jnp.bfloat16)


def draw_qkv_weight(key, part):
    key = jax.random.fold_in(key, 12)
    first_key = jax.random.fold_in(key, 0)
    width_all = HEADS * HD
    normal_part = jnp.clip(jax.random.normal(first_key, (D, 3 * width_all), jnp.float32), -6.0, 6.0)
    return (normal_part / D ** 0.5).astype(jnp.bfloat16)


def draw_node_order(key, part):
    key = jax.random.fold_in(key, 13)
    part_keys = jax.random.split(key, N_DOM)

    def shuffled(part_key):
        return jax.random.permutation(part_key, NPART).astype(jnp.int32)
    local = jax.vmap(shuffled)(part_keys)
    offsets = jnp.arange(N_DOM, dtype=jnp.int32)[:, None] * NPART
    return (local + offsets).reshape(-1).astype(jnp.int32)


def draw_row_count(key, part):
    key = jax.random.fold_in(key, 14)
    count_key, spot_key = jax.random.split(key, 2)
    counts = jax.random.randint(count_key, (N_DOM * BLOCKS,), BLK // 8, BLK + 1, jnp.int32)
    spot = jax.random.randint(spot_key, (), 0, N_DOM * BLOCKS, jnp.int32)
    return jnp.where(jnp.arange(N_DOM * BLOCKS, dtype=jnp.int32) == spot, BLK, counts).astype(jnp.int32)


def touch_ends(entries, rng, least, top_value):
    longest = entries.shape.index(max(entries.shape))
    spots = []
    for shift in (0, 1):
        where = [jax.random.randint(jax.random.fold_in(rng, axis), (), 0, length) for axis, length in enumerate(entries.shape)]
        where[longest] = (where[longest] + shift) % entries.shape[longest]
        spots.append(tuple(where))
    return entries.at[spots[0]].set(least).at[spots[1]].set(top_value)


def block_levels(own_key, extent, pieces, low, largest):
    def one(axis_at, blocks):
        draws = jax.random.uniform(jax.random.fold_in(jax.random.fold_in(own_key, 6), axis_at), (blocks,), jnp.float32, low / len(pieces), largest / len(pieces))
        return jnp.repeat(jnp.exp(draws), extent[axis_at] // blocks).reshape((-1,) + (1,) * (len(extent) - axis_at - 1))

    level = one(*pieces[0])
    for cut in pieces[1:]:
        level = level * one(*cut)
    return level


def shared_out(own_key, own, number, rows, number_of, top, limit, lean):
    order = jax.random.permutation(own_key, number_of)
    crowded, ordinary = load_shares(number_of, rows * top, limit, lean, True), load_shares(number_of, rows * top, limit, lean, False)
    places = jnp.arange(number_of)

    def named(sizes, rotation):
        used = int((sizes > 0).sum())
        fixed = max(1, used // 4)
        moved = fixed + (places - fixed + rotation * (used - fixed)) % max(1, number_of - fixed)
        return jnp.zeros((number_of,), jnp.int32).at[order[jnp.where(places < fixed, places, moved)]].set(jnp.asarray(sizes, jnp.int32))

    sizes = jnp.where(number % 4 == 0, named(crowded, number // 4), named(ordinary, number - number // 4 - 1))
    mixed = jax.random.permutation(jax.random.fold_in(own, 3), number_of)
    donor, taker = mixed[0:number_of // 2 * 2:2], mixed[1:number_of // 2 * 2:2]
    slack = jnp.minimum(sizes[donor] - 1, limit - sizes[taker]) // 2
    slack = jnp.where((donor == order[0]) | (taker == order[0]) | (sizes[taker] == 0), 0, jnp.maximum(slack, 0))
    moved = jax.random.randint(jax.random.fold_in(own, 4), (number_of // 2,), 0, 1 << 20) % (slack + 1)
    sizes = sizes.at[donor].add(-moved).at[taker].add(moved)
    items = jnp.searchsorted(jnp.cumsum(sizes), jnp.arange(rows * top), side="right").astype(jnp.int32)
    listing = items.reshape(top, rows).T
    listing = listing[jax.random.permutation(jax.random.fold_in(own, 1), rows)]
    rotation = jax.random.randint(jax.random.fold_in(own, 2), (rows, 1), 0, top)
    return jnp.take_along_axis(listing, (jnp.arange(top)[None, :] + rotation) % top, axis=1)


def load_shares(amount, total, reach, skew, full):
    portions = [(1 << 20) // math.isqrt(grade ** skew) + 1 for grade in range(1, amount + 1)]
    largest = reach if full else min(reach, max(-(-total // amount), total * portions[0] // sum(portions)))
    least = 1 if total - largest >= amount - 1 else 0
    holding, spare = [largest] + [least] * (amount - 1), total - largest - least * (amount - 1)
    while spare > 0:
        free = [i for i in range(1, amount) if holding[i] < largest] or [i for i in range(1, amount) if holding[i] < reach]
        mass, remaining = sum([portions[i] for i in free]), spare
        for i in free:
            extra = min(reach - holding[i], max(1, remaining * portions[i] // mass), spare)
            holding[i] = holding[i] + extra
            spare = spare - extra
    return np.array(holding)


def centred(stream_key, extent, scale, most, cuts=(), kind=jnp.bfloat16):
    values = scale * jax.random.normal(stream_key, extent, jnp.float32)
    if cuts:
        values = values * block_levels(stream_key, extent, cuts, -0.22, 0.18)
    return jnp.clip(values, -most, most).astype(kind)


def setup_inputs(seed: int = 0) -> dict:
    splits = jax.random.split(jax.random.key(seed), 12)
    features = draw_features(jax.random.fold_in(splits[11], 71), 0)
    qkv_weight = draw_qkv_weight(jax.random.fold_in(splits[11], 71), 0)
    out_weight = centred(splits[2], (HEADS * HD, D), (HEADS * HD) ** -0.5, 0.25)
    attn_gain = jnp.clip(1.0 + 0.18 * jax.random.normal(splits[3], (D,), jnp.float32), 0.1, 1.9)
    up_weight = centred(splits[4], (D, FF), D ** -0.5, 0.21875, ((1, 64),))
    down_weight = centred(splits[5], (FF, D), FF ** -0.5, 0.15625, ((0, 64),))
    final_gain = jnp.clip(1.0 + 0.18 * jax.random.normal(splits[6], (D,), jnp.float32), 0.1, 1.9)
    node_order = draw_node_order(jax.random.fold_in(splits[11], 71), 0)
    dest_part_keys = jax.random.split(jax.random.fold_in(splits[8], 1), (N_DOM * BLOCKS) // BLOCKS)
    dest_part_turns = jax.random.permutation(jax.random.fold_in(splits[8], 3), (N_DOM * BLOCKS) // BLOCKS)
    dest_part = jax.vmap(lambda own, number: shared_out(jax.random.fold_in(splits[8], 2), own, number, BLOCKS, N_DOM, TOP, CAP, 2))(dest_part_keys, dest_part_turns).reshape((N_DOM * BLOCKS, TOP))
    key_block = touch_ends(jax.random.randint(splits[9], (N_DOM * BLOCKS, TOP), 0, BLOCKS), jax.random.fold_in(splits[9], 1), 0, BLOCKS - 1).astype(jnp.int32)
    row_count = draw_row_count(jax.random.fold_in(splits[11], 71), 0)
    return dict(features=features, qkv_weight=qkv_weight, out_weight=out_weight, attn_gain=attn_gain, up_weight=up_weight, down_weight=down_weight, final_gain=final_gain, node_order=node_order, dest_part=dest_part, key_block=key_block, row_count=row_count)


def layer_norm(values, gain):
    centered = values - lax.optimization_barrier(jnp.mean(values, -1, keepdims=True))
    spread = lax.optimization_barrier(jnp.mean(centered * centered, -1, keepdims=True))
    return centered * lax.rsqrt(spread + 1e-05) * gain

def pair_attention(query_rep, key_list, value_list, key_count):
    head_width = query_rep.shape[-1]
    scores = jnp.einsum('pqhe,pkhe->phqk', query_rep.astype(jnp.float32), key_list.astype(jnp.float32)) * (1.0 / math.sqrt(head_width))
    positions = jnp.arange(key_list.shape[1], dtype=jnp.int32)
    kept_keys = positions[None, :] < key_count[:, None]
    scores = jnp.where(kept_keys[:, None, None, :], scores, -1e+30)
    maxima = lax.optimization_barrier(jnp.max(scores, -1))
    weights = jnp.exp(scores - maxima[..., None])
    totals = lax.optimization_barrier(jnp.sum(weights, -1))
    probs = weights.astype(jnp.bfloat16).astype(jnp.float32)
    summed = jnp.einsum('phqk,pkhe->pqhe', probs, value_list.astype(jnp.float32))
    partial_out = (summed / jnp.transpose(totals, (0, 2, 1))[..., None]).astype(jnp.bfloat16)
    return (maxima, totals, partial_out)

def reference(features, qkv_weight, out_weight, attn_gain, up_weight, down_weight, final_gain, node_order, dest_part, key_block, row_count):
    width_all = HEADS * HD
    qkv = jnp.dot(features, qkv_weight, preferred_element_type=jnp.float32).astype(jnp.bfloat16)
    clustered = qkv[node_order]
    total_blocks = N_DOM * BLOCKS
    queries = clustered[:, :width_all].reshape(total_blocks, BLK, HEADS, HD)
    keys_all = clustered[:, width_all:2 * width_all].reshape(total_blocks, BLK, HEADS, HD)
    values_all = clustered[:, 2 * width_all:].reshape(total_blocks, BLK, HEADS, HD)
    own_ids = jnp.arange(total_blocks, dtype=jnp.int32)
    lists = jnp.concatenate([own_ids[:, None], (dest_part * BLOCKS + key_block).astype(jnp.int32)], 1)

    def block_attention(query_one, list_one, own_count):
        key_list = keys_all[list_one]
        value_list = values_all[list_one]
        query_rep = jnp.broadcast_to(query_one[None], key_list.shape)
        maxima, totals, partial_out = pair_attention(query_rep, key_list, value_list, row_count[list_one])
        top_peak = lax.optimization_barrier(jnp.max(maxima, 0))
        scale = totals * jnp.exp(maxima - top_peak[None])
        numer = lax.optimization_barrier(jnp.sum(partial_out.astype(jnp.float32) * jnp.transpose(scale, (0, 2, 1))[..., None], 0))
        denom = jnp.transpose(lax.optimization_barrier(jnp.sum(scale, 0)), (1, 0))[..., None]
        merged = numer / denom
        valid = jnp.arange(BLK, dtype=jnp.int32) < own_count
        return jnp.where(valid[:, None, None], merged, 0.0).astype(jnp.bfloat16)
    groups = total_blocks // 8

    def one_group(packed):
        return jax.vmap(block_attention)(packed[0], packed[1], packed[2])
    attended = lax.map(one_group, (queries.reshape(groups, 8, BLK, HEADS, HD), lists.reshape(groups, 8, TOP + 1), row_count.reshape(groups, 8)))
    attended = attended.reshape(NODES, width_all)
    attention = jnp.zeros((NODES, width_all), jnp.bfloat16).at[node_order].set(attended)
    residual_sum = features.astype(jnp.float32) + jnp.dot(attention, out_weight, preferred_element_type=jnp.float32)
    hidden_norm = layer_norm(residual_sum, attn_gain).astype(jnp.bfloat16)
    hidden = jax.nn.gelu(jnp.dot(hidden_norm, up_weight, preferred_element_type=jnp.float32)).astype(jnp.bfloat16)
    mixed = hidden_norm.astype(jnp.float32) + jnp.dot(hidden, down_weight, preferred_element_type=jnp.float32)
    return layer_norm(mixed, final_gain).astype(jnp.bfloat16)
```

```python
import functools

import jax
import jax.numpy as jnp
from jax import lax
from jax.experimental import pallas as pl
from jax.experimental.pallas import tpu as pltpu
from jax.sharding import PartitionSpec as P

HEADS = 8
HD = 64
BLK = 128
NZ = 16
NX = 4
PART = BLK // HEADS
HALF_RING = NZ // 2
FULL_HOPS = 4
MESH = pl.DeviceIdType.MESH
VMEM = pl.BlockSpec(memory_space=pltpu.VMEM)
SMEM = pl.BlockSpec(memory_space=pltpu.SMEM)
ANY = pl.BlockSpec(memory_space=pl.ANY)
LIMIT = 60 * 1024 * 1024


def greet(partners):
    barrier = pltpu.get_barrier_semaphore()
    for partner in partners:
        pl.semaphore_signal(barrier, inc=1, device_id=partner, device_id_type=MESH)
    pl.semaphore_wait(barrier, len(partners))


def send(source, target, send_sem, recv_sem, partner):
    copy = pltpu.make_async_remote_copy(
        src_ref=source,
        dst_ref=target,
        send_sem=send_sem,
        recv_sem=recv_sem,
        device_id=partner,
        device_id_type=MESH,
    )
    copy.start()
    return copy


def cluster_kernel(
    features,
    picked,
    extra,
    own_table,
    carried,
    tables,
    weights,
    pool,
    total,
    send_sem,
    recv_sem,
    table_send,
    table_recv,
    ring_send,
    ring_recv,
    local_sem,
):
    dom, head = lax.axis_index("dom"), lax.axis_index("head")
    z, x = dom // NX, lax.rem(dom, NX)
    y, core = head // 2, lax.rem(head, 2)

    def at(step, other):
        return lax.rem(y + step, 4) * 2 + lax.rem(core + other, 2)

    right, left, peer = {"head": at(1, 0)}, {"head": at(3, 0)}, {"head": at(0, 1)}
    planes = [None] + [{"dom": lax.rem(z + step, NZ) * NX + x} for step in range(1, NZ)]
    columns = [None] + [{"dom": z * NX + lax.rem(x + step, NX)} for step in range(1, NX)]
    greet([right, left, peer] + planes[1:] + columns[1:])
    started = []

    def put(*operands):
        started.append(send(*operands))
        return started[-1]

    rows = features.shape[0]
    half = rows // 2
    upper, lower = pl.ds(0, half), pl.ds(half, half)

    def go(number, source, slot, part, partner):
        target = pool.at[slot] if part is None else pool.at[slot, part]
        return put(source, target, send_sem.at[number], recv_sem.at[number], partner)

    def weights_go(direction, hop):
        place = HALF_RING * direction + hop
        return put(
            extra if hop == 1 else weights.at[place - 1],
            weights.at[place],
            ring_send.at[place],
            ring_recv.at[place],
            planes[1] if direction == 0 else planes[NZ - 1],
        )

    right_a = go(0, features.at[upper], 1, upper, right)
    left_b = go(1, features.at[lower], 2, lower, left)
    right_b = go(2, features.at[lower], 1, lower, right)
    left_a = go(3, features.at[upper], 2, upper, left)
    own_peer = go(4, features, 4, None, peer)
    hops = [weights_go(0, 1), weights_go(1, 1)]
    table_x = [
        put(own_table, tables.at[pl.ds(dom, 1)], table_send.at[step], table_recv.at[step], columns[step])
        for step in range(1, NX)
    ]
    own_weights = pltpu.make_async_copy(extra, weights.at[0], local_sem.at[0])
    own_weights.start()
    own_row = pltpu.make_async_copy(own_table, tables.at[pl.ds(dom, 1)], local_sem.at[1])
    own_row.start()

    row_ids = lax.broadcasted_iota(jnp.int32, (rows, rows), 1)
    wanted = picked[...]

    def add(block, owner, first=False):
        chosen = jnp.where(wanted - owner * rows == row_ids, 1.0, 0.0).astype(jnp.bfloat16)
        product = jnp.dot(chosen, block, preferred_element_type=jnp.float32)
        total[...] = product if first else total[...] + product

    def weights_on(hop):
        for direction in range(2):
            if hops[direction] is not None:
                hops[direction].wait_recv()
                last = hop == HALF_RING - direction
                hops[direction] = None if last else weights_go(direction, hop + 1)

    own_row.wait()
    for copy in table_x:
        copy.wait_recv()
    plane_rows = tables.at[pl.ds(z * NX, NX)]
    table_z = [
        put(plane_rows, plane_rows, table_send.at[NX + step], table_recv.at[NX + step], planes[step])
        for step in range(1, NZ)
    ]
    add(features[...], head, True)
    weights_on(1)
    right_a.wait_recv()
    on_a = go(5, pool.at[1, upper], 3, upper, right)
    left_b.wait_recv()
    on_b = go(6, pool.at[2, lower], 3, lower, left)
    weights_on(2)
    own_peer.wait_recv()
    add(pool[4], at(0, 1))
    weights_on(3)
    right_b.wait_recv()
    from_left = go(7, pool.at[1], 5, None, peer)
    left_a.wait_recv()
    from_right = go(8, pool.at[2], 6, None, peer)
    weights_on(4)
    add(pool[1], at(3, 0))
    weights_on(5)
    add(pool[2], at(1, 0))
    weights_on(6)
    from_left.wait_recv()
    add(pool[5], at(3, 1))
    weights_on(7)
    from_right.wait_recv()
    add(pool[6], at(1, 1))
    weights_on(8)
    on_a.wait_recv()
    on_b.wait_recv()
    across = go(9, pool.at[3], 7, None, peer)
    add(pool[3], at(2, 0))
    across.wait_recv()
    add(pool[7], at(2, 1))
    carried[...] = total[...].astype(jnp.bfloat16).reshape(rows // PART, PART, features.shape[1])
    for copy in table_z:
        copy.wait_recv()
    own_weights.wait()
    for copy in started:
        copy.wait_send()


def cluster(features, picked, extra, own_table):
    rows, width = features.shape
    dma = pltpu.SemaphoreType.DMA
    return pl.pallas_call(
        cluster_kernel,
        out_shape=(
            jax.ShapeDtypeStruct((rows // PART, PART, width), jnp.bfloat16),
            jax.ShapeDtypeStruct((NZ * NX,) + own_table.shape[1:], jnp.int32),
            jax.ShapeDtypeStruct((NZ,) + extra.shape, jnp.bfloat16),
        ),
        in_specs=[VMEM, VMEM, VMEM, VMEM],
        out_specs=(VMEM, VMEM, VMEM),
        scratch_shapes=[
            pltpu.VMEM((8, rows, width), jnp.bfloat16),
            pltpu.VMEM((rows, width), jnp.float32),
            dma((10,)),
            dma((10,)),
            dma((NX + NZ,)),
            dma((NX + NZ,)),
            dma((NZ,)),
            dma((NZ,)),
            dma((2,)),
        ],
        compiler_params=pltpu.CompilerParams(
            collective_id=1, has_side_effects=True, vmem_limit_bytes=LIMIT
        ),
        name="cluster_rows",
    )(features, picked, extra, own_table)


def hop_size(hop):
    return 32 if hop <= FULL_HOPS else 4 + 8 * (HALF_RING - hop)


def slot_base(step):
    return 0 if step == 0 else 8 + 16 * (step - 1)


def ring_kernel(
    wanted,
    carried,
    qkv_weight,
    weight_column,
    own_query,
    own_pair,
    slot_pair,
    weights,
    *scratch,
):
    full = scratch[: 2 * FULL_HOPS]
    ring_body(
        wanted,
        carried,
        qkv_weight,
        weight_column,
        own_query,
        own_pair,
        slot_pair,
        weights,
        full,
        *scratch[2 * FULL_HOPS :],
    )


def ring_body(
    wanted,
    carried,
    qkv_weight,
    weight_column,
    own_query,
    own_pair,
    slot_pair,
    weights,
    full,
    part_way,
    trimmed,
    picked,
    arrived,
    sent_own,
    sent_slot,
    ring_send,
    ring_recv,
    row_send,
    row_recv,
    spread_send,
    spread_recv,
    weight_send,
    weight_recv,
    own_send,
    own_recv,
    peer_send,
    peer_recv,
):
    dom, head = lax.axis_index("dom"), lax.axis_index("head")
    z, x = dom // NX, lax.rem(dom, NX)
    core = lax.rem(head, 2)
    width = carried.shape[2]

    def plane(step):
        return lax.rem(z + step + NZ, NZ)

    def column(step):
        return lax.rem(x + step, NX)

    up = {"dom": plane(1) * NX + x}
    down = {"dom": plane(-1) * NX + x}
    rows_x = [None] + [{"dom": z * NX + column(step)} for step in range(1, NX)]
    heads = [None] + [{"head": lax.rem(head + step, HEADS)} for step in range(1, HEADS)]
    peer = {"head": head + 1 - 2 * core}
    greet([up, down] + rows_x[1:] + heads[1:])
    started, locals_started = [], []

    def landing(direction, hop):
        if hop <= FULL_HOPS:
            return full[FULL_HOPS * direction + hop - 1]
        return part_way.at[direction, hop - FULL_HOPS - 1]

    def source_of(direction, hop):
        if hop == 1:
            return carried
        if hop == FULL_HOPS + 1:
            return trimmed.at[direction]
        return landing(direction, hop - 1)

    def parts_of(hop):
        size = hop_size(hop)
        if hop == HALF_RING:
            return [(0, size)]
        middle = size // 2
        return [(0, middle), (middle, size - middle)]

    def ring_go(direction, hop, part):
        first, count = parts_of(hop)[part]
        copy = send(
            source_of(direction, hop).at[pl.ds(first, count)],
            landing(direction, hop).at[pl.ds(first, count)],
            ring_send.at[direction, hop - 1, part],
            ring_recv.at[direction, hop - 1, part],
            up if direction == 0 else down,
        )
        started.append(copy)
        return copy

    def listed(plane_step, column_id, source, turn):
        return wanted[plane(plane_step) * NX + column_id, 0, 2 * source + turn]

    weight_copies = []

    def weights_along(step):
        if step:
            copy = send(
                weight_column,
                weights.at[core, NX - step],
                weight_send.at[step],
                weight_recv.at[step],
                rows_x[step],
            )
            started.append(copy)
        else:
            copy = pltpu.make_async_copy(weight_column, weights.at[core, 0], weight_send.at[0])
            copy.start()
        weight_copies.append(copy)

    slot_copies = {step: [] for step in range(HALF_RING + 1)}

    def slots_from_full(chunk, source, step, direction, buffer):
        base = slot_base(step) + 8 * direction
        for turn in range(2):
            arrived[base + turn] = chunk[listed(0, x, source, turn)]
        for along in range(1, NX):
            for turn in range(2):
                picked[buffer, along - 1, turn] = chunk[listed(0, column(along), source, turn)]
            copy = send(
                picked.at[buffer, along - 1],
                arrived.at[pl.ds(base + 2 * (NX - along), 2)],
                row_send.at[step, direction, along],
                row_recv.at[step, direction, along],
                rows_x[along],
            )
            started.append(copy)
            slot_copies[step].append(copy)

    def slots_from_trimmed(chunk, step, direction):
        if step == HALF_RING:
            first, count, base = 0, 1, slot_base(step) + direction
        else:
            first, count, base = 4 + 8 * (HALF_RING - 1 - step), 2, slot_base(step) + 8 * direction
        arrived[pl.ds(base, count)] = chunk[pl.ds(first + count * x, count)]
        for along in range(1, NX):
            copy = send(
                chunk.at[pl.ds(first + count * column(along), count)],
                arrived.at[pl.ds(base + 2 * (NX - along), count)],
                row_send.at[step, direction, along],
                row_recv.at[step, direction, along],
                rows_x[along],
            )
            started.append(copy)
            slot_copies[step].append(copy)

    def spread(source, target, number, send_sem, recv_sem, base, count):
        copies = []
        for step in range(1, HEADS):
            other = lax.rem(head + step, HEADS)
            copy = send(
                source.at[other, pl.ds(base, count)],
                target.at[pl.ds(base, count), head],
                send_sem.at[number, step],
                recv_sem.at[number, step],
                heads[step],
            )
            started.append(copy)
            copies.append(copy)
        copy = pltpu.make_async_copy(
            source.at[head, pl.ds(base, count)],
            target.at[pl.ds(base, count), head],
            send_sem.at[number, 0],
        )
        copy.start()
        locals_started.append(copy)
        return copies

    spread_copies = []

    def peer_weights():
        weight_copies[0].wait()
        for copy in weight_copies[1:]:
            copy.wait_recv()
        copy = send(weights.at[core], weights.at[core], peer_send, peer_recv, peer)
        started.append(copy)
        spread_copies.append(copy)

    lower_lanes = lax.broadcasted_iota(jnp.int32, (16 * PART, BLK), 1) < HD

    def store_pairs(rows, target, base):
        count = rows.shape[0] // PART
        width_all = HEADS * HD
        keys = jnp.dot(
            rows, qkv_weight[:, width_all : 2 * width_all], preferred_element_type=jnp.float32
        )
        values = jnp.dot(
            rows, qkv_weight[:, 2 * width_all :], preferred_element_type=jnp.float32
        )
        lower = lower_lanes[: rows.shape[0]]
        for pair in range(HEADS // 2):
            lanes = slice(pair * BLK, (pair + 1) * BLK)
            key, value = keys[:, lanes], values[:, lanes]
            even = jnp.where(lower, value, pltpu.roll(key, HD, 1))
            odd = jnp.where(lower, pltpu.roll(value, HD, 1), key)
            for other, tile in ((2 * pair, even), (2 * pair + 1, odd)):
                target[other, pl.ds(base, count)] = tile.astype(jnp.bfloat16).reshape(
                    count, PART, BLK
                )

    def store_queries(rows, target, base):
        count = rows.shape[0] // PART
        queries = jnp.dot(rows, qkv_weight[:, : HEADS * HD], preferred_element_type=jnp.float32)
        queries = queries * (HD**-0.5)
        lower = lower_lanes[: rows.shape[0]]
        for pair in range(HEADS // 2):
            query = queries[:, pair * BLK : (pair + 1) * BLK]
            even = jnp.where(lower, 0.0, pltpu.roll(query, HD, 1))
            odd = jnp.where(lower, 0.0, query)
            for other, tile in ((2 * pair, even), (2 * pair + 1, odd)):
                target[other, pl.ds(base, count)] = tile.astype(jnp.bfloat16).reshape(
                    count, PART, BLK
                )

    def project(step):
        count = 16 if 0 < step < HALF_RING else 8
        base = slot_base(step)
        for copy in slot_copies[step]:
            copy.wait_recv()
        rows = arrived[pl.ds(base, count)].reshape(count * PART, width)
        store_pairs(rows, sent_slot, base)
        spread_copies.extend(
            spread(sent_slot, slot_pair, step, spread_send, spread_recv, base, count)
        )

    ring = {}
    for part in range(2):
        for direction in range(2):
            ring[direction, 1, part] = ring_go(direction, 1, part)
    slots_from_full(carried, dom, 0, 0, 0)

    @pl.loop(0, 2)
    def _(half):
        rows = carried[pl.ds(16 * half, 16)].reshape(16 * PART, width)
        store_queries(rows, sent_own.at[0], 16 * half)
        store_pairs(rows, sent_own.at[1], 16 * half)

    spread_copies.extend(spread(sent_own.at[0], own_query, 0, own_send, own_recv, 0, 32))
    spread_copies.extend(spread(sent_own.at[1], own_pair, 1, own_send, own_recv, 0, 32))

    for hop in range(1, HALF_RING + 1):
        last = hop == HALF_RING
        sources = [plane(-hop) * NX + x, plane(hop) * NX + x]
        for direction in range(2):
            ring[direction, hop, 0].wait_recv()
            if not last and hop != FULL_HOPS:
                ring[direction, hop + 1, 0] = ring_go(direction, hop + 1, 0)
        if not last:
            project(hop - 1)
            for direction in range(2):
                ring[direction, hop, 1].wait_recv()
                if hop != FULL_HOPS:
                    if (direction, hop + 1, 1) not in ring and hop + 1 < HALF_RING:
                        ring[direction, hop + 1, 1] = ring_go(direction, hop + 1, 1)
        if hop == FULL_HOPS:
            for direction in range(2):
                sign = 1 if direction == 0 else -1
                chunk = landing(direction, hop)
                for column_id in range(NX):
                    trimmed[direction, column_id] = chunk[
                        listed(sign * (HALF_RING - hop), column_id, sources[direction], direction)
                    ]
                for ahead in range(HALF_RING - hop - 1, 0, -1):
                    first = 4 + 8 * (HALF_RING - hop - 1 - ahead)
                    for column_id in range(NX):
                        for turn in range(2):
                            trimmed[direction, first + 2 * column_id + turn] = chunk[
                                listed(sign * ahead, column_id, sources[direction], turn)
                            ]
                for part in range(2):
                    ring[direction, hop + 1, part] = ring_go(direction, hop + 1, part)
        for direction in range(2):
            chunk = landing(direction, hop)
            if hop <= FULL_HOPS:
                slots_from_full(
                    chunk, sources[direction], hop, direction, 1 + 2 * (hop - 1) + direction
                )
            else:
                slots_from_trimmed(chunk, hop, direction)
        if hop <= NX:
            weights_along(hop - 1)
        if hop == HALF_RING - 1:
            peer_weights()
    project(HALF_RING - 1)
    project(HALF_RING)
    for copy in spread_copies:
        copy.wait_recv()
    for copy in started:
        copy.wait_send()
    for copy in locals_started:
        copy.wait()


def ring(wanted, carried, qkv_weight, weight_column):
    width = carried.shape[2]
    bf16 = jnp.bfloat16
    dma = pltpu.SemaphoreType.DMA
    return pl.pallas_call(
        ring_kernel,
        out_shape=(
            jax.ShapeDtypeStruct((32, HEADS, PART, BLK), bf16),
            jax.ShapeDtypeStruct((32, HEADS, PART, BLK), bf16),
            jax.ShapeDtypeStruct((128, HEADS, PART, BLK), bf16),
            jax.ShapeDtypeStruct((2, NX) + weight_column.shape, bf16),
        ),
        in_specs=[SMEM, VMEM, VMEM, VMEM],
        out_specs=(ANY, ANY, ANY, ANY),
        scratch_shapes=[pltpu.VMEM(carried.shape, bf16)] * (2 * FULL_HOPS)
        + [
            pltpu.VMEM((2, HALF_RING - FULL_HOPS, hop_size(FULL_HOPS + 1), PART, width), bf16),
            pltpu.VMEM((2, hop_size(FULL_HOPS + 1), PART, width), bf16),
            pltpu.VMEM((1 + 2 * FULL_HOPS, NX - 1, 2, PART, width), bf16),
            pltpu.VMEM((128, PART, width), bf16),
            pltpu.VMEM((2, HEADS, 32, PART, BLK), bf16),
            pltpu.VMEM((HEADS, 128, PART, BLK), bf16),
            dma((2, HALF_RING, 2)),
            dma((2, HALF_RING, 2)),
            dma((HALF_RING + 1, 2, NX)),
            dma((HALF_RING + 1, 2, NX)),
            dma((HALF_RING + 1, HEADS)),
            dma((HALF_RING + 1, HEADS)),
            dma((NX,)),
            dma((NX,)),
            dma((2, HEADS)),
            dma((2, HEADS)),
            dma,
            dma,
        ],
        compiler_params=pltpu.CompilerParams(
            collective_id=2, has_side_effects=True, vmem_limit_bytes=LIMIT
        ),
        name="ring_blocks",
    )(wanted, carried, qkv_weight, weight_column)


def attend_kernel(slots, counts, order, query, own_pair, slot_pair, out, held, merged):
    key_ids = lax.broadcasted_iota(jnp.int32, (BLK, BLK), 1)
    row_ids = lax.broadcasted_iota(jnp.int32, (BLK, BLK), 0)

    def one(block, place):
        queries = query[block]
        pairs = [own_pair[block], slot_pair[slots[2 * block]], slot_pair[slots[2 * block + 1]]]
        scores = []
        for turn, pair in enumerate(pairs):
            score = lax.dot_general(
                queries, pair, (((1,), (1,)), ((), ())), preferred_element_type=jnp.float32
            )
            scores.append(jnp.where(key_ids < counts[3 * block + turn], score, -1e30))
        peak = jnp.max(jnp.maximum(jnp.maximum(scores[0], scores[1]), scores[2]), 1, keepdims=True)
        weights = [jnp.exp(score - peak) for score in scores]
        total = jnp.sum(weights[0] + weights[1] + weights[2], 1, keepdims=True)
        summed = sum(
            jnp.dot(weight.astype(jnp.bfloat16), pair, preferred_element_type=jnp.float32)
            for weight, pair in zip(weights, pairs)
        )
        merged[place] = jnp.where(row_ids < counts[3 * block], summed / total, 0.0)

    @pl.loop(0, 16)
    def _(step):
        one(2 * step, 0)
        one(2 * step + 1, 1)

        @pl.loop(0, 16)
        def _(piece):
            for place in range(2):
                rows = merged[place, pl.ds(pl.multiple_of(8 * piece, 8), 8)]
                for row in range(8):
                    target = order[256 * step + 128 * place + 8 * piece + row]
                    held[pl.ds(target, 1), :] = rows[row : row + 1, :]

    out[...] = held[:, :HD].astype(jnp.bfloat16)


def attend(slots, counts, order, query, own_pair, slot_pair):
    rows = order.shape[0]
    return pl.pallas_call(
        attend_kernel,
        out_shape=jax.ShapeDtypeStruct((rows, HD), jnp.bfloat16),
        in_specs=[SMEM, SMEM, SMEM, VMEM, VMEM, VMEM],
        out_specs=VMEM,
        scratch_shapes=[
            pltpu.VMEM((rows, BLK), jnp.float32),
            pltpu.VMEM((2, BLK, BLK), jnp.float32),
        ],
        compiler_params=pltpu.CompilerParams(vmem_limit_bytes=LIMIT),
        name="attend_blocks",
    )(slots, counts, order, query, own_pair, slot_pair)


def regroup_kernel(attended, grouped, send_sem, recv_sem, local_sem):
    head = lax.axis_index("head")
    others = [lax.rem(head + step, HEADS) for step in range(1, HEADS)]
    greet([{"head": other} for other in others])
    copies = []
    for step, other in enumerate(others):
        copies.append(
            send(
                attended.at[other],
                grouped.at[head],
                send_sem.at[step],
                recv_sem.at[step],
                {"head": other},
            )
        )
    own = pltpu.make_async_copy(attended.at[head], grouped.at[head], local_sem)
    own.start()
    own.wait()
    for copy in copies:
        copy.wait()


def regroup(attended):
    return pl.pallas_call(
        regroup_kernel,
        out_shape=jax.ShapeDtypeStruct(attended.shape, attended.dtype),
        in_specs=[VMEM],
        out_specs=VMEM,
        scratch_shapes=[
            pltpu.SemaphoreType.DMA((HEADS - 1,)),
            pltpu.SemaphoreType.DMA((HEADS - 1,)),
            pltpu.SemaphoreType.DMA,
        ],
        compiler_params=pltpu.CompilerParams(
            collective_id=3, has_side_effects=True, vmem_limit_bytes=LIMIT
        ),
        name="regroup_heads",
    )(attended)


def layer_norm(values, gain):
    centered = values - jnp.mean(values, -1, keepdims=True)
    spread = jnp.mean(centered * centered, -1, keepdims=True)
    return centered * lax.rsqrt(spread + 1e-05) * gain


def tail_kernel(features, grouped, out_weight, attn_gain, weights, final_gain, out, mixed):
    attention = jnp.dot(grouped[0], out_weight[0], preferred_element_type=jnp.float32)
    for head in range(1, HEADS):
        attention += jnp.dot(grouped[head], out_weight[head], preferred_element_type=jnp.float32)
    residual_sum = features[...].astype(jnp.float32) + attention
    hidden_norm = layer_norm(residual_sum, attn_gain[...]).astype(jnp.bfloat16)
    mixed[...] = hidden_norm.astype(jnp.float32)
    tile = 512

    @pl.loop(0, weights.shape[1] // tile)
    def _(step):
        units = pl.ds(pl.multiple_of(step * tile, tile), tile)
        hidden = lax.dot_general(
            hidden_norm,
            weights[0, units],
            (((1,), (1,)), ((), ())),
            preferred_element_type=jnp.float32,
        )
        hidden = jax.nn.gelu(hidden).astype(jnp.bfloat16)
        mixed[...] += jnp.dot(hidden, weights[1, units], preferred_element_type=jnp.float32)

    out[...] = layer_norm(mixed[...], final_gain[...]).astype(jnp.bfloat16)


def tail(features, grouped, out_weight, attn_gain, weights, final_gain):
    return pl.pallas_call(
        tail_kernel,
        out_shape=jax.ShapeDtypeStruct(features.shape, jnp.bfloat16),
        in_specs=[VMEM] * 6,
        out_specs=VMEM,
        scratch_shapes=[pltpu.VMEM(features.shape, jnp.float32)],
        compiler_params=pltpu.CompilerParams(vmem_limit_bytes=LIMIT),
        name="tail_rows",
    )(features, grouped, out_weight, attn_gain, weights, final_gain)


def per_device(
    features,
    qkv_weight,
    out_weight,
    attn_gain,
    up_weight,
    down_weight,
    final_gain,
    node_order,
    dest_part,
    key_block,
    row_count,
):
    blocks, listed = dest_part.shape
    partitions = NZ * NX
    width = features.shape[1]
    dom, head = lax.axis_index("dom"), lax.axis_index("head")
    core = head % 2
    bf16 = jnp.bfloat16

    dest_flat, block_flat = dest_part.reshape(-1), key_block.reshape(-1)
    names = dest_flat[:, None] == jnp.arange(partitions, dtype=jnp.int32)[None, :]
    earlier = jnp.tril(dest_flat[:, None] == dest_flat[None, :], -1)
    turn = jnp.sum(earlier.astype(jnp.int32), 1)
    chosen = names[:, :, None] & (turn[:, None, None] == jnp.arange(2, dtype=jnp.int32))
    wanted = jnp.sum(jnp.where(chosen, block_flat[:, None, None], 0), 0).reshape(1, -1)
    own_table = jnp.stack([wanted[0], jnp.pad(row_count, (0, wanted.shape[1] - blocks))])[None]

    npart = node_order.shape[0]
    local_order = node_order - dom * npart
    picked = lax.dynamic_index_in_dim(
        local_order.reshape(blocks, HEADS, PART), head, 1, keepdims=False
    ).reshape(-1, 1)
    extra = jnp.where(core == 0, up_weight.T, down_weight)
    extra = jnp.pad(extra, ((0, 2 * PART - extra.shape[0]), (0, 0))).reshape(2, PART, width)
    carried, tables, weight_column = cluster(features, picked, extra, own_table)
    own_query, own_pair, slot_pair, weights = ring(tables, carried, qkv_weight, weight_column)

    z, x = dom // NX, dom % NX
    gap = (z - dest_flat // NX) % NZ
    across = (dest_flat % NX - x) % NX
    start = jnp.where(
        gap == 0,
        0,
        jnp.where(gap <= HALF_RING, 8 + 16 * (gap - 1), 8 + 16 * (NZ - gap - 1) + 8),
    )
    slots = start + 2 * across + turn
    listed_rows = tables[:, 1, :blocks].reshape(-1)[dest_flat * blocks + block_flat]
    counts = jnp.concatenate([row_count[:, None], listed_rows.reshape(blocks, listed)], 1)

    attended = attend(
        slots,
        counts.reshape(-1),
        local_order,
        own_query.reshape(blocks, BLK, BLK),
        own_pair.reshape(blocks, BLK, BLK),
        slot_pair.reshape(2 * partitions, BLK, BLK),
    )
    grouped = regroup(attended.reshape(HEADS, npart // HEADS, HD))
    return tail(
        features,
        grouped,
        out_weight.reshape(HEADS, HD, width),
        attn_gain.reshape(1, width),
        weights.reshape(2, partitions * 2 * PART, width),
        final_gain.reshape(1, width),
    )


def solution(mesh):
    in_specs = (
        P(("dom", "head"), None),
        P(),
        P(),
        P(),
        P(None, "dom"),
        P("dom", None),
        P(),
        P("dom"),
        P("dom", None),
        P("dom", None),
        P("dom"),
    )
    out_specs = P(("dom", "head"), None)
    return jax.shard_map(
        per_device, mesh=mesh, in_specs=in_specs, out_specs=out_specs, check_vma=False
    )
```

```python
import functools

import jax
import jax.numpy as jnp
from jax import lax
from jax.experimental import pallas as pl
from jax.experimental.pallas import tpu as pltpu
from jax.sharding import PartitionSpec as P

HEADS = 8
HD = 64
BLK = 128
NZ = 16
NX = 4
PART = BLK // HEADS
HALF_RING = NZ // 2
FULL_HOPS = 4
MESH = pl.DeviceIdType.MESH
VMEM = pl.BlockSpec(memory_space=pltpu.VMEM)
SMEM = pl.BlockSpec(memory_space=pltpu.SMEM)
ANY = pl.BlockSpec(memory_space=pl.ANY)
LIMIT = 60 * 1024 * 1024


def greet(partners):
    barrier = pltpu.get_barrier_semaphore()
    for partner in partners:
        pl.semaphore_signal(barrier, inc=1, device_id=partner, device_id_type=MESH)
    pl.semaphore_wait(barrier, len(partners))


def send(source, target, send_sem, recv_sem, partner):
    copy = pltpu.make_async_remote_copy(
        src_ref=source,
        dst_ref=target,
        send_sem=send_sem,
        recv_sem=recv_sem,
        device_id=partner,
        device_id_type=MESH,
    )
    copy.start()
    return copy


def hop_size(hop):
    return 32 if hop <= FULL_HOPS else 4 + 8 * (HALF_RING - hop)


def slot_base(step):
    return 0 if step == 0 else 8 + 16 * (step - 1)


def exchange_kernel(*refs):
    inputs, outputs, scratch = refs[:7], refs[7:12], refs[12:]
    whole = 4 * FULL_HOPS + 2
    exchange_body(*inputs, *outputs, scratch[:2], scratch[2:whole], *scratch[whole:])


def exchange_body(
    features,
    picked,
    up_rows,
    down_rows,
    wanted_row,
    count_row,
    qkv_weight,
    own_query,
    own_pair,
    slot_pair,
    weights,
    tables,
    carried,
    full,
    pool,
    total,
    extra,
    own_table,
    weight_column,
    wanted,
    part_way,
    trimmed,
    chosen,
    arrived,
    sent_own,
    sent_slot,
    pool_send,
    pool_recv,
    table_send,
    table_recv,
    column_send,
    column_recv,
    ring_send,
    ring_recv,
    row_send,
    row_recv,
    spread_send,
    spread_recv,
    weight_send,
    weight_recv,
    own_send,
    own_recv,
    peer_send,
    peer_recv,
    local_sem,
):
    dom, head = lax.axis_index("dom"), lax.axis_index("head")
    z, x = dom // NX, lax.rem(dom, NX)
    y, core = head // 2, lax.rem(head, 2)
    rows, width = features.shape
    part_width = width // 2

    def plane(step):
        return lax.rem(z + step + NZ, NZ)

    def column(step):
        return lax.rem(x + step, NX)

    def at(step, other):
        return lax.rem(y + step, 4) * 2 + lax.rem(core + other, 2)

    planes = [None] + [{"dom": plane(step) * NX + x} for step in range(1, NZ)]
    rows_x = [None] + [{"dom": z * NX + column(step)} for step in range(1, NX)]
    heads = [None] + [{"head": lax.rem(head + step, HEADS)} for step in range(1, HEADS)]
    right, left, peer = {"head": at(1, 0)}, {"head": at(3, 0)}, {"head": at(0, 1)}
    up, down = planes[1], planes[NZ - 1]
    greet(planes[1:] + rows_x[1:] + heads[1:])
    started, locals_started = [], []

    def put(*operands):
        started.append(send(*operands))
        return started[-1]

    def local(source, target, number):
        copy = pltpu.make_async_copy(source, target, local_sem.at[number])
        copy.start()
        return copy

    half = rows // 2
    upper, lower = pl.ds(0, half), pl.ds(half, half)

    def pool_go(part, number, source, slot, which, partner):
        target = pool.at[part, slot] if which is None else pool.at[part, slot, which]
        return put(source, target, pool_send.at[part, number], pool_recv.at[part, number], partner)

    def pool_own(part):
        lanes = pl.ds(part * part_width, part_width)
        return {
            "right_a": pool_go(part, 0, features.at[upper, lanes], 1, upper, right),
            "left_b": pool_go(part, 1, features.at[lower, lanes], 2, lower, left),
            "right_b": pool_go(part, 2, features.at[lower, lanes], 1, lower, right),
            "left_a": pool_go(part, 3, features.at[upper, lanes], 2, upper, left),
            "own_peer": pool_go(part, 4, features.at[:, lanes], 4, None, peer),
        }

    def weights_go(direction, hop):
        place = HALF_RING * direction + hop
        return put(
            extra if hop == 1 else weight_column.at[place - 1],
            weight_column.at[place],
            column_send.at[place],
            column_recv.at[place],
            up if direction == 0 else down,
        )

    first_pool = pool_own(0)
    own_table[0, :, : wanted_row.shape[1]] = wanted_row[...]
    own_table[0, :, wanted_row.shape[1] :] = count_row[...]
    table_x = [
        put(own_table, tables.at[pl.ds(dom, 1)], table_send.at[step], table_recv.at[step], rows_x[step])
        for step in range(1, NX)
    ]
    own_row = local(own_table, tables.at[pl.ds(dom, 1)], 0)
    units = jnp.where(core == 0, up_rows[...], down_rows[...])
    filler = jnp.zeros((2 * PART - units.shape[0], width), units.dtype)
    extra[...] = jnp.concatenate([units, filler], 0).reshape(2, PART, width)
    hops = [weights_go(0, 1), weights_go(1, 1)]
    own_weights = local(extra, weight_column.at[0], 1)

    def weights_on(hop):
        for direction in range(2):
            if hops[direction] is not None:
                hops[direction].wait_recv()
                last = hop == HALF_RING - direction
                hops[direction] = None if last else weights_go(direction, hop + 1)

    row_ids = lax.broadcasted_iota(jnp.int32, (rows, rows), 1)
    picks = picked[...]

    def add(block, owner, first=False):
        hit = jnp.where(picks - owner * rows == row_ids, 1.0, 0.0).astype(jnp.bfloat16)
        product = jnp.dot(hit, block, preferred_element_type=jnp.float32)
        total[...] = product if first else total[...] + product

    def gather_rows(part, got, along):
        add(features[:, part * part_width : (part + 1) * part_width], head, True)
        got["right_a"].wait_recv()
        on_a = pool_go(part, 5, pool.at[part, 1, upper], 3, upper, right)
        got["left_b"].wait_recv()
        on_b = pool_go(part, 6, pool.at[part, 2, lower], 3, lower, left)
        along(0)
        got["own_peer"].wait_recv()
        add(pool[part, 4], at(0, 1))
        along(1)
        got["right_b"].wait_recv()
        from_left = pool_go(part, 7, pool.at[part, 1], 5, None, peer)
        got["left_a"].wait_recv()
        from_right = pool_go(part, 8, pool.at[part, 2], 6, None, peer)
        along(2)
        add(pool[part, 1], at(3, 0))
        along(3)
        add(pool[part, 2], at(1, 0))
        along(4)
        from_left.wait_recv()
        add(pool[part, 5], at(3, 1))
        along(5)
        from_right.wait_recv()
        add(pool[part, 6], at(1, 1))
        along(6)
        on_a.wait_recv()
        on_b.wait_recv()
        across = pool_go(part, 9, pool.at[part, 3], 7, None, peer)
        add(pool[part, 3], at(2, 0))
        along(7)
        across.wait_recv()
        add(pool[part, 7], at(2, 1))
        carried[part][...] = (
            total[...].astype(jnp.bfloat16).reshape(rows // PART, PART, part_width)
        )

    def landing(direction, hop, part):
        if hop <= FULL_HOPS:
            return full[4 * (hop - 1) + 2 * direction + part]
        return part_way.at[direction, hop - FULL_HOPS - 1, part]

    def ring_go(direction, hop, part):
        if hop == 1:
            source = carried[part]
        elif hop == FULL_HOPS + 1:
            source = trimmed.at[direction, part]
        else:
            source = landing(direction, hop - 1, part)
        count = pl.ds(0, hop_size(hop))
        ring[direction, hop, part] = put(
            source.at[count],
            landing(direction, hop, part).at[count],
            ring_send.at[direction, hop - 1, part],
            ring_recv.at[direction, hop - 1, part],
            up if direction == 0 else down,
        )

    def listed(plane_step, column_id, source, turn):
        return wanted[plane(plane_step) * NX + column_id, 0, 2 * source + turn]

    def trim(direction, part):
        chunk = landing(direction, FULL_HOPS, part)
        sign = 1 if direction == 0 else -1
        source = plane(-sign * FULL_HOPS) * NX + x
        beyond = HALF_RING - FULL_HOPS
        for column_id in range(NX):
            trimmed[direction, part, column_id] = chunk[
                listed(sign * beyond, column_id, source, direction)
            ]
        for ahead in range(beyond - 1, 0, -1):
            first = 4 + 8 * (beyond - 1 - ahead)
            for column_id in range(NX):
                for turn in range(2):
                    trimmed[direction, part, first + 2 * column_id + turn] = chunk[
                        listed(sign * ahead, column_id, source, turn)
                    ]

    slot_copies = {step: [] for step in range(HALF_RING + 1)}

    def slot_go(source, base, step, direction, part, along, count):
        slot_copies[step].append(
            put(
                source,
                arrived.at[part, pl.ds(base + 2 * (NX - along), count)],
                row_send.at[step, direction, part, along],
                row_recv.at[step, direction, part, along],
                rows_x[along],
            )
        )

    def slots_along(step, direction, part):
        base = slot_base(step) + 8 * direction
        if step <= FULL_HOPS:
            chunk = landing(direction, step, part) if step else carried[part]
            source = plane(-step if direction == 0 else step) * NX + x
            buffer = 2 * step - 1 + direction if step else 0
            for turn in range(2):
                arrived[part, base + turn] = chunk[listed(0, x, source, turn)]
            for along in range(1, NX):
                for turn in range(2):
                    chosen[buffer, part, along - 1, turn] = chunk[
                        listed(0, column(along), source, turn)
                    ]
                slot_go(chosen.at[buffer, part, along - 1], base, step, direction, part, along, 2)
            return
        chunk = landing(direction, step, part)
        if step == HALF_RING:
            first, count, base = 0, 1, slot_base(step) + direction
        else:
            first, count = 4 + 8 * (HALF_RING - 1 - step), 2
        arrived[part, pl.ds(base, count)] = chunk[pl.ds(first + count * x, count)]
        for along in range(1, NX):
            source = chunk.at[pl.ds(first + count * column(along), count)]
            slot_go(source, base, step, direction, part, along, count)

    weight_copies, spread_copies = [], []

    def weights_along(step):
        if step:
            weight_copies.append(
                put(
                    weight_column,
                    weights.at[core, NX - step],
                    weight_send.at[step],
                    weight_recv.at[step],
                    rows_x[step],
                )
            )
        else:
            weight_copies.append(local(weight_column, weights.at[core, 0], 2))

    def peer_weights():
        weight_copies[0].wait()
        for copy in weight_copies[1:]:
            copy.wait_recv()
        spread_copies.append(put(weights.at[core], weights.at[core], peer_send, peer_recv, peer))

    def spread(source, target, number, send_sem, recv_sem, base, count):
        for step in range(1, HEADS):
            other = lax.rem(head + step, HEADS)
            spread_copies.append(
                put(
                    source.at[other, pl.ds(base, count)],
                    target.at[pl.ds(base, count), head],
                    send_sem.at[number, step],
                    recv_sem.at[number, step],
                    heads[step],
                )
            )
        copy = pltpu.make_async_copy(
            source.at[head, pl.ds(base, count)],
            target.at[pl.ds(base, count), head],
            send_sem.at[number, 0],
        )
        copy.start()
        locals_started.append(copy)

    lower_lanes = lax.broadcasted_iota(jnp.int32, (16 * PART, BLK), 1) < HD

    def store_tile(tile, target, other, base):
        count = tile.shape[0] // PART
        target[other, pl.ds(base, count)] = tile.astype(jnp.bfloat16).reshape(count, PART, BLK)

    def store_pairs(values_in, target, base):
        width_all = HEADS * HD
        keys = jnp.dot(
            values_in, qkv_weight[:, width_all : 2 * width_all], preferred_element_type=jnp.float32
        )
        values = jnp.dot(
            values_in, qkv_weight[:, 2 * width_all :], preferred_element_type=jnp.float32
        )
        is_lower = lower_lanes[: values_in.shape[0]]
        for pair in range(HEADS // 2):
            lanes = slice(pair * BLK, (pair + 1) * BLK)
            key, value = keys[:, lanes], values[:, lanes]
            even = jnp.where(is_lower, value, pltpu.roll(key, HD, 1))
            odd = jnp.where(is_lower, pltpu.roll(value, HD, 1), key)
            store_tile(even, target, 2 * pair, base)
            store_tile(odd, target, 2 * pair + 1, base)

    def store_queries(values_in, target, base):
        queries = jnp.dot(
            values_in, qkv_weight[:, : HEADS * HD], preferred_element_type=jnp.float32
        )
        queries = queries * (HD**-0.5)
        is_lower = lower_lanes[: values_in.shape[0]]
        for pair in range(HEADS // 2):
            query = queries[:, pair * BLK : (pair + 1) * BLK]
            store_tile(jnp.where(is_lower, 0.0, pltpu.roll(query, HD, 1)), target, 2 * pair, base)
            store_tile(jnp.where(is_lower, 0.0, query), target, 2 * pair + 1, base)

    def project_own():
        @pl.loop(0, 2)
        def _(step):
            blocks = pl.ds(16 * step, 16)
            joined = jnp.concatenate(
                [carried[part][blocks].reshape(16 * PART, part_width) for part in range(2)], 1
            )
            store_queries(joined, sent_own.at[0], 16 * step)
            store_pairs(joined, sent_own.at[1], 16 * step)

        spread(sent_own.at[0], own_query, 0, own_send, own_recv, 0, 32)
        spread(sent_own.at[1], own_pair, 1, own_send, own_recv, 0, 32)

    def project(step):
        count = 16 if 0 < step < HALF_RING else 8
        base = slot_base(step)
        for copy in slot_copies[step]:
            copy.wait_recv()
        joined = jnp.concatenate(
            [
                arrived[part, pl.ds(base, count)].reshape(count * PART, part_width)
                for part in range(2)
            ],
            1,
        )
        store_pairs(joined, sent_slot, base)
        spread(sent_slot, slot_pair, step, spread_send, spread_recv, base, count)

    ring, pools, table_z = {}, [first_pool], []

    def during_first(moment):
        if moment == 0:
            pools.append(pool_own(1))
            own_row.wait()
            for copy in table_x:
                copy.wait_recv()
            plane_rows = tables.at[pl.ds(z * NX, NX)]
            for step in range(1, NZ):
                table_z.append(
                    put(
                        plane_rows,
                        plane_rows,
                        table_send.at[NX + step],
                        table_recv.at[NX + step],
                        planes[step],
                    )
                )
        weights_on(moment + 1)

    gather_rows(0, pools[0], during_first)
    for direction in range(2):
        ring_go(direction, 1, 0)
    for copy in table_z:
        copy.wait_recv()
    local(tables, wanted, 3).wait()
    slots_along(0, 0, 0)
    gather_rows(1, pools[1], lambda moment: None)
    for direction in range(2):
        ring_go(direction, 1, 1)
    slots_along(0, 0, 1)
    own_weights.wait()

    for hop in range(1, HALF_RING + 1):
        for part in range(2):
            for direction in range(2):
                ring[direction, hop, part].wait_recv()
                if hop == FULL_HOPS:
                    trim(direction, part)
                if hop < HALF_RING:
                    ring_go(direction, hop + 1, part)
            for direction in range(2):
                slots_along(hop, direction, part)
            if hop == 1 and part == 0:
                project_own()
        if hop <= NX:
            weights_along(hop - 1)
        if hop == HALF_RING - 1:
            peer_weights()
        project(hop - 1)
    project(HALF_RING)
    for copy in spread_copies:
        copy.wait_recv()
    for copy in started:
        copy.wait_send()
    for copy in locals_started:
        copy.wait()


def exchange(features, picked, up_rows, down_rows, wanted_row, count_row, qkv_weight):
    rows, width = features.shape
    blocks, part_width = rows // PART, width // 2
    bf16 = jnp.bfloat16
    dma = pltpu.SemaphoreType.DMA
    tables = (NZ * NX, 1, 2 * wanted_row.shape[1])
    return pl.pallas_call(
        exchange_kernel,
        out_shape=(
            jax.ShapeDtypeStruct((blocks, HEADS, PART, BLK), bf16),
            jax.ShapeDtypeStruct((blocks, HEADS, PART, BLK), bf16),
            jax.ShapeDtypeStruct((2 * NZ * NX, HEADS, PART, BLK), bf16),
            jax.ShapeDtypeStruct((2, NX, NZ, 2, PART, width), bf16),
            jax.ShapeDtypeStruct(tables, jnp.int32),
        ),
        in_specs=[VMEM] * 7,
        out_specs=(ANY, ANY, ANY, ANY, ANY),
        scratch_shapes=[pltpu.VMEM((blocks, PART, part_width), bf16)] * (2 + 4 * FULL_HOPS)
        + [
            pltpu.VMEM((2, 8, rows, part_width), bf16),
            pltpu.VMEM((rows, part_width), jnp.float32),
            pltpu.VMEM((2, PART, width), bf16),
            pltpu.VMEM((1,) + tables[1:], jnp.int32),
            pltpu.VMEM((NZ, 2, PART, width), bf16),
            pltpu.SMEM(tables, jnp.int32),
            pltpu.VMEM(
                (2, HALF_RING - FULL_HOPS, 2, hop_size(FULL_HOPS + 1), PART, part_width), bf16
            ),
            pltpu.VMEM((2, 2, hop_size(FULL_HOPS + 1), PART, part_width), bf16),
            pltpu.VMEM((1 + 2 * FULL_HOPS, 2, NX - 1, 2, PART, part_width), bf16),
            pltpu.VMEM((2, 2 * NZ * NX, PART, part_width), bf16),
            pltpu.VMEM((2, HEADS, blocks, PART, BLK), bf16),
            pltpu.VMEM((HEADS, 2 * NZ * NX, PART, BLK), bf16),
            dma((2, 10)),
            dma((2, 10)),
            dma((NX + NZ,)),
            dma((NX + NZ,)),
            dma((NZ,)),
            dma((NZ,)),
            dma((2, HALF_RING, 2)),
            dma((2, HALF_RING, 2)),
            dma((HALF_RING + 1, 2, 2, NX)),
            dma((HALF_RING + 1, 2, 2, NX)),
            dma((HALF_RING + 1, HEADS)),
            dma((HALF_RING + 1, HEADS)),
            dma((NX,)),
            dma((NX,)),
            dma((2, HEADS)),
            dma((2, HEADS)),
            dma,
            dma,
            dma((4,)),
        ],
        compiler_params=pltpu.CompilerParams(
            collective_id=1, has_side_effects=True, vmem_limit_bytes=LIMIT
        ),
        name="exchange_blocks",
    )(features, picked, up_rows, down_rows, wanted_row, count_row, qkv_weight)


def attend_kernel(
    dest, key_block, turn, row_count, tables, order, query, own_pair, slot_pair, out, held, *merged
):
    key_ids = lax.broadcasted_iota(jnp.int32, (BLK, BLK), 1)
    row_ids = lax.broadcasted_iota(jnp.int32, (BLK, BLK), 0)
    dom = lax.axis_index("dom")
    z, x = dom // NX, lax.rem(dom, NX)
    node_base = dom * order.shape[0]

    def slot_of(entry):
        owner = dest[entry]
        gap = lax.rem(z - owner // NX + NZ, NZ)
        start = jnp.where(gap <= HALF_RING, 16 * gap - 8, 16 * (NZ - gap))
        start = jnp.where(gap == 0, 0, start)
        across = lax.rem(lax.rem(owner, NX) - x + NX, NX)
        return start + 2 * across + turn[entry], tables[owner, 0, 2 * NZ * NX + key_block[entry]]

    def one(block, target):
        queries = query[block]
        first, first_count = slot_of(2 * block)
        second, second_count = slot_of(2 * block + 1)
        own_count = row_count[block]
        pairs = [own_pair[block], slot_pair[first], slot_pair[second]]
        scores = []
        for pair, count in zip(pairs, (own_count, first_count, second_count)):
            score = lax.dot_general(
                queries, pair, (((1,), (1,)), ((), ())), preferred_element_type=jnp.float32
            )
            scores.append(jnp.where(key_ids < count, score, -1e30))
        peak = jnp.max(jnp.maximum(jnp.maximum(scores[0], scores[1]), scores[2]), 1, keepdims=True)
        weights = [jnp.exp(score - peak) for score in scores]
        total = jnp.sum(weights[0] + weights[1] + weights[2], 1, keepdims=True)
        summed = sum(
            jnp.dot(weight.astype(jnp.bfloat16), pair, preferred_element_type=jnp.float32)
            for weight, pair in zip(weights, pairs)
        )
        target[...] = jnp.where(row_ids < own_count, summed / total, 0.0)

    def place(block, source):
        for piece in range(BLK // 8):
            values = source[pl.ds(8 * piece, 8)]
            for row in range(8):
                node = order[BLK * block + 8 * piece + row] - node_base
                held[pl.ds(node, 1), :] = values[row : row + 1, :]

    blocks = query.shape[0]

    @pl.loop(0, blocks // 4)
    def _(step):
        for side in range(2):
            pair = 2 * step + side
            before = lax.rem(pair + blocks // 2 - 1, blocks // 2)
            for number in range(2):
                one(2 * pair + number, merged[2 * side + number])
                place(2 * before + number, merged[2 * (1 - side) + number])

    for number in range(2):
        place(blocks - 2 + number, merged[2 + number])
    half = BLK * blocks // HEADS // 2
    is_lower = lax.broadcasted_iota(jnp.int32, (half, BLK), 1) < HD
    for owner in range(HEADS):
        first = held[pl.ds(2 * half * owner, half)]
        second = held[pl.ds(2 * half * owner + half, half)]
        out[owner] = jnp.where(is_lower, first, pltpu.roll(second, HD, 1)).astype(jnp.bfloat16)


def attend(dest, key_block, turn, row_count, tables, order, query, own_pair, slot_pair):
    rows = order.shape[0]
    return pl.pallas_call(
        attend_kernel,
        out_shape=jax.ShapeDtypeStruct((HEADS, rows // HEADS // 2, BLK), jnp.bfloat16),
        in_specs=[SMEM] * 6 + [VMEM] * 3,
        out_specs=VMEM,
        scratch_shapes=[pltpu.VMEM((rows, BLK), jnp.float32)]
        + [pltpu.VMEM((BLK, BLK), jnp.float32)] * 4,
        compiler_params=pltpu.CompilerParams(vmem_limit_bytes=LIMIT),
        name="attend_blocks",
    )(dest, key_block, turn, row_count, tables, order, query, own_pair, slot_pair)


def layer_norm(values, gain):
    centered = values - jnp.mean(values, -1, keepdims=True)
    spread = jnp.mean(centered * centered, -1, keepdims=True)
    return centered * lax.rsqrt(spread + 1e-05) * gain


def finish_kernel(
    features,
    attended,
    out_weight,
    attn_gain,
    weights,
    final_gain,
    out,
    grouped,
    spaced,
    units,
    mixed,
    send_sem,
    recv_sem,
    local_sem,
):
    head = lax.axis_index("head")
    others = [lax.rem(head + step, HEADS) for step in range(1, HEADS)]
    greet([{"head": other} for other in others])
    copies = [
        send(
            attended.at[other], grouped.at[head], send_sem.at[step], recv_sem.at[step], {"head": other}
        )
        for step, other in enumerate(others)
    ]
    own = pltpu.make_async_copy(attended.at[head], grouped.at[head], local_sem.at[0])
    own.start()
    load = pltpu.make_async_copy(weights, units, local_sem.at[1])
    load.start()
    gap = jnp.zeros((HD, out_weight.shape[1]), out_weight.dtype)
    for number in range(HEADS):
        block = out_weight[pl.ds(HD * number, HD)]
        for side in range(2):
            spaced[side, pl.ds(BLK * number + HD * side, HD)] = block
            spaced[side, pl.ds(BLK * number + HD * (1 - side), HD)] = gap
    own.wait()
    for copy in copies:
        copy.wait()
    joined = jnp.concatenate([grouped[number] for number in range(HEADS)], 1)
    half = joined.shape[0]
    for side in range(2):
        part = pl.ds(side * half, half)
        attention = jnp.dot(joined, spaced[side], preferred_element_type=jnp.float32)
        residual_sum = features[part].astype(jnp.float32) + attention
        mixed[part] = layer_norm(residual_sum, attn_gain[...])
    hidden_norm = mixed[...].astype(jnp.bfloat16)
    mixed[...] = hidden_norm.astype(jnp.float32)
    load.wait()
    tile = 512
    for step in range(units.shape[1] // tile):
        here = pl.ds(step * tile, tile)
        hidden = lax.dot_general(
            hidden_norm,
            units[0, here],
            (((1,), (1,)), ((), ())),
            preferred_element_type=jnp.float32,
        )
        hidden = jax.nn.gelu(hidden).astype(jnp.bfloat16)
        mixed[...] += jnp.dot(hidden, units[1, here], preferred_element_type=jnp.float32)
    out[...] = layer_norm(mixed[...], final_gain[...]).astype(jnp.bfloat16)


def finish(features, attended, out_weight, attn_gain, weights, final_gain):
    dma = pltpu.SemaphoreType.DMA
    return pl.pallas_call(
        finish_kernel,
        out_shape=jax.ShapeDtypeStruct(features.shape, jnp.bfloat16),
        in_specs=[VMEM] * 4 + [ANY, VMEM],
        out_specs=VMEM,
        scratch_shapes=[
            pltpu.VMEM(attended.shape, jnp.bfloat16),
            pltpu.VMEM((2, HEADS * BLK, features.shape[1]), jnp.bfloat16),
            pltpu.VMEM(weights.shape, jnp.bfloat16),
            pltpu.VMEM(features.shape, jnp.float32),
            dma((HEADS - 1,)),
            dma((HEADS - 1,)),
            dma((2,)),
        ],
        compiler_params=pltpu.CompilerParams(
            collective_id=2, has_side_effects=True, vmem_limit_bytes=LIMIT
        ),
        name="finish_rows",
    )(features, attended, out_weight, attn_gain, weights, final_gain)


def per_device(
    features,
    qkv_weight,
    out_weight,
    attn_gain,
    up_weight,
    down_weight,
    final_gain,
    node_order,
    dest_part,
    key_block,
    row_count,
):
    blocks = dest_part.shape[0]
    partitions = NZ * NX
    width = features.shape[1]
    dom, head = lax.axis_index("dom"), lax.axis_index("head")

    dest_flat, block_flat = dest_part.reshape(-1), key_block.reshape(-1)
    names = dest_flat[:, None] == jnp.arange(partitions, dtype=jnp.int32)[None, :]
    earlier = jnp.tril(dest_flat[:, None] == dest_flat[None, :], -1)
    turn = jnp.sum(earlier.astype(jnp.int32), 1)
    chosen = names[:, :, None] & (turn[:, None, None] == jnp.arange(2, dtype=jnp.int32))
    wanted = jnp.sum(jnp.where(chosen, block_flat[:, None, None], 0), 0).reshape(1, -1)

    picked = lax.dynamic_index_in_dim(
        node_order.reshape(blocks, HEADS, PART), head, 1, keepdims=False
    ).reshape(-1, 1)
    picked = picked - dom * node_order.shape[0]
    own_query, own_pair, slot_pair, weights, tables = exchange(
        features,
        picked,
        up_weight.T,
        down_weight,
        wanted,
        jnp.pad(row_count, (0, wanted.shape[1] - blocks)).reshape(1, -1),
        qkv_weight,
    )
    attended = attend(
        dest_flat,
        block_flat,
        turn,
        row_count,
        tables,
        node_order,
        own_query.reshape(blocks, BLK, BLK),
        own_pair.reshape(blocks, BLK, BLK),
        slot_pair.reshape(2 * partitions, BLK, BLK),
    )
    return finish(
        features,
        attended,
        out_weight,
        attn_gain.reshape(1, width),
        weights.reshape(2, partitions * 2 * PART, width),
        final_gain.reshape(1, width),
    )


def solution(mesh):
    in_specs = (
        P(("dom", "head"), None),
        P(),
        P(),
        P(),
        P(None, "dom"),
        P("dom", None),
        P(),
        P("dom"),
        P("dom", None),
        P("dom", None),
        P("dom"),
    )
    out_specs = P(("dom", "head"), None)
    return jax.shard_map(
        per_device, mesh=mesh, in_specs=in_specs, out_specs=out_specs, check_vma=False
    )
```

```python
import functools

import jax
import jax.numpy as jnp
from jax import lax
from jax.experimental import pallas as pl
from jax.experimental.pallas import tpu as pltpu
from jax.sharding import PartitionSpec as P

HEADS = 8
HD = 64
BLK = 128
NZ = 16
NX = 4
PART = BLK // HEADS
HALF_RING = NZ // 2
FULL_HOPS = 4
PARTS = 3
MESH = pl.DeviceIdType.MESH
VMEM = pl.BlockSpec(memory_space=pltpu.VMEM)
SMEM = pl.BlockSpec(memory_space=pltpu.SMEM)
ANY = pl.BlockSpec(memory_space=pl.ANY)
LIMIT = 60 * 1024 * 1024


def greet(partners):
    barrier = pltpu.get_barrier_semaphore()
    for partner in partners:
        pl.semaphore_signal(barrier, inc=1, device_id=partner, device_id_type=MESH)
    pl.semaphore_wait(barrier, len(partners))


def send(source, target, send_sem, recv_sem, partner):
    copy = pltpu.make_async_remote_copy(
        src_ref=source,
        dst_ref=target,
        send_sem=send_sem,
        recv_sem=recv_sem,
        device_id=partner,
        device_id_type=MESH,
    )
    copy.start()
    return copy


def hop_size(hop):
    return 32 if hop <= FULL_HOPS else 4 + 8 * (HALF_RING - hop)


def slot_base(step):
    return 0 if step == 0 else 8 + 16 * (step - 1)


def exchange_kernel(*refs):
    inputs, outputs, scratch = refs[:7], refs[7:12], refs[12:]
    whole = (2 * FULL_HOPS + 1) * PARTS
    exchange_body(*inputs, *outputs, scratch[:PARTS], scratch[PARTS:whole], *scratch[whole:])


def exchange_body(
    features,
    picked,
    up_rows,
    down_rows,
    wanted_row,
    count_row,
    qkv_weight,
    own_query,
    own_pair,
    slot_pair,
    weights,
    tables,
    carried,
    full,
    pool,
    total,
    extra,
    own_table,
    weight_column,
    wanted,
    part_way,
    trimmed,
    chosen,
    arrived,
    sent_own,
    sent_slot,
    pool_send,
    pool_recv,
    table_send,
    table_recv,
    column_send,
    column_recv,
    ring_send,
    ring_recv,
    row_send,
    row_recv,
    spread_send,
    spread_recv,
    weight_send,
    weight_recv,
    own_send,
    own_recv,
    peer_send,
    peer_recv,
    local_sem,
):
    dom, head = lax.axis_index("dom"), lax.axis_index("head")
    z, x = dom // NX, lax.rem(dom, NX)
    y, core = head // 2, lax.rem(head, 2)
    rows, width = features.shape
    part_width = width // PARTS

    def plane(step):
        return lax.rem(z + step + NZ, NZ)

    def column(step):
        return lax.rem(x + step, NX)

    def at(step, other):
        return lax.rem(y + step, 4) * 2 + lax.rem(core + other, 2)

    planes = [None] + [{"dom": plane(step) * NX + x} for step in range(1, NZ)]
    rows_x = [None] + [{"dom": z * NX + column(step)} for step in range(1, NX)]
    heads = [None] + [{"head": lax.rem(head + step, HEADS)} for step in range(1, HEADS)]
    right, left, peer = {"head": at(1, 0)}, {"head": at(3, 0)}, {"head": at(0, 1)}
    up, down = planes[1], planes[NZ - 1]
    greet(planes[1:] + rows_x[1:] + heads[1:])
    started, locals_started = [], []

    def put(*operands):
        started.append(send(*operands))
        return started[-1]

    def local(source, target, number):
        copy = pltpu.make_async_copy(source, target, local_sem.at[number])
        copy.start()
        return copy

    half = rows // 2
    upper, lower = pl.ds(0, half), pl.ds(half, half)

    def pool_go(part, number, source, slot, which, partner):
        target = pool.at[part, slot] if which is None else pool.at[part, slot, which]
        return put(source, target, pool_send.at[part, number], pool_recv.at[part, number], partner)

    def pool_own(part):
        lanes = pl.ds(part * part_width, part_width)
        return {
            "right_a": pool_go(part, 0, features.at[upper, lanes], 1, upper, right),
            "left_b": pool_go(part, 1, features.at[lower, lanes], 2, lower, left),
            "right_b": pool_go(part, 2, features.at[lower, lanes], 1, lower, right),
            "left_a": pool_go(part, 3, features.at[upper, lanes], 2, upper, left),
            "own_peer": pool_go(part, 4, features.at[:, lanes], 4, None, peer),
        }

    def weights_go(direction, hop):
        place = HALF_RING * direction + hop
        return put(
            extra if hop == 1 else weight_column.at[place - 1],
            weight_column.at[place],
            column_send.at[place],
            column_recv.at[place],
            up if direction == 0 else down,
        )

    first_pool = pool_own(0)
    own_table[0, :, : wanted_row.shape[1]] = wanted_row[...]
    own_table[0, :, wanted_row.shape[1] :] = jnp.zeros_like(wanted_row)
    own_table[0, :, pl.ds(wanted_row.shape[1], count_row.shape[1])] = count_row[...]
    table_x = [
        put(own_table, tables.at[pl.ds(dom, 1)], table_send.at[step], table_recv.at[step], rows_x[step])
        for step in range(1, NX)
    ]
    own_row = local(own_table, tables.at[pl.ds(dom, 1)], 0)
    units = jnp.where(core == 0, up_rows[...], down_rows[...])
    filler = jnp.zeros((2 * PART - units.shape[0], width), units.dtype)
    extra[...] = jnp.concatenate([units, filler], 0).reshape(2, PART, width)
    hops = [weights_go(0, 1), weights_go(1, 1)]
    own_weights = local(extra, weight_column.at[0], 1)

    def weights_on(hop):
        for direction in range(2):
            if hops[direction] is not None:
                hops[direction].wait_recv()
                last = hop == HALF_RING - direction
                hops[direction] = None if last else weights_go(direction, hop + 1)

    row_ids = lax.broadcasted_iota(jnp.int32, (rows, rows), 1)
    picks = picked[...]

    def add(block, owner, first=False):
        hit = jnp.where(picks - owner * rows == row_ids, 1.0, 0.0).astype(jnp.bfloat16)
        product = jnp.dot(hit, block, preferred_element_type=jnp.float32)
        total[...] = product if first else total[...] + product

    def gather_rows(part, got, along):
        add(features[:, part * part_width : (part + 1) * part_width], head, True)
        got["right_a"].wait_recv()
        on_a = pool_go(part, 5, pool.at[part, 1, upper], 3, upper, right)
        got["left_b"].wait_recv()
        on_b = pool_go(part, 6, pool.at[part, 2, lower], 3, lower, left)
        along(0)
        got["own_peer"].wait_recv()
        add(pool[part, 4], at(0, 1))
        along(1)
        got["right_b"].wait_recv()
        from_left = pool_go(part, 7, pool.at[part, 1], 5, None, peer)
        got["left_a"].wait_recv()
        from_right = pool_go(part, 8, pool.at[part, 2], 6, None, peer)
        along(2)
        add(pool[part, 1], at(3, 0))
        along(3)
        add(pool[part, 2], at(1, 0))
        along(4)
        from_left.wait_recv()
        add(pool[part, 5], at(3, 1))
        along(5)
        from_right.wait_recv()
        add(pool[part, 6], at(1, 1))
        along(6)
        on_a.wait_recv()
        on_b.wait_recv()
        across = pool_go(part, 9, pool.at[part, 3], 7, None, peer)
        add(pool[part, 3], at(2, 0))
        along(7)
        across.wait_recv()
        add(pool[part, 7], at(2, 1))
        carried[part][...] = (
            total[...].astype(jnp.bfloat16).reshape(rows // PART, PART, part_width)
        )

    def landing(direction, hop, part):
        if hop <= FULL_HOPS:
            return full[PARTS * (2 * (hop - 1) + direction) + part]
        return part_way.at[direction, hop - FULL_HOPS - 1, part]

    def ring_go(direction, hop, part):
        if hop == 1:
            source = carried[part]
        elif hop == FULL_HOPS + 1:
            source = trimmed.at[direction, part]
        else:
            source = landing(direction, hop - 1, part)
        count = pl.ds(0, hop_size(hop))
        ring[direction, hop, part] = put(
            source.at[count],
            landing(direction, hop, part).at[count],
            ring_send.at[direction, hop - 1, part],
            ring_recv.at[direction, hop - 1, part],
            up if direction == 0 else down,
        )

    def listed(plane_step, column_id, source, turn):
        return wanted[plane(plane_step) * NX + column_id, 0, 2 * source + turn]

    def trim(direction, part):
        chunk = landing(direction, FULL_HOPS, part)
        sign = 1 if direction == 0 else -1
        source = plane(-sign * FULL_HOPS) * NX + x
        beyond = HALF_RING - FULL_HOPS
        for column_id in range(NX):
            trimmed[direction, part, column_id] = chunk[
                listed(sign * beyond, column_id, source, direction)
            ]
        for ahead in range(beyond - 1, 0, -1):
            first = 4 + 8 * (beyond - 1 - ahead)
            for column_id in range(NX):
                for turn in range(2):
                    trimmed[direction, part, first + 2 * column_id + turn] = chunk[
                        listed(sign * ahead, column_id, source, turn)
                    ]

    slot_copies = {step: [] for step in range(HALF_RING + 1)}

    def slots_pick(step, direction, part):
        base = slot_base(step) + 8 * direction
        chunk = landing(direction, step, part) if step else carried[part]
        source = plane(-step if direction == 0 else step) * NX + x
        buffer = 2 * step - 1 + direction if step else 0
        for turn in range(2):
            arrived[part, base + turn] = chunk[listed(0, x, source, turn)]
        for along in range(1, NX):
            for turn in range(2):
                chosen[buffer, along - 1, part, turn] = chunk[
                    listed(0, column(along), source, turn)
                ]

    def slots_along(step, direction):
        count, base = 2, slot_base(step) + 8 * direction
        if step > FULL_HOPS:
            chunk = part_way.at[direction, step - FULL_HOPS - 1]
            first = 4 + 8 * (HALF_RING - 1 - step)
            if step == HALF_RING:
                first, count, base = 0, 1, slot_base(step) + direction
            arrived[:, pl.ds(base, count)] = chunk[:, pl.ds(first + count * x, count)]
        for along in range(1, NX):
            if step > FULL_HOPS:
                source = chunk.at[:, pl.ds(first + count * column(along), count)]
            else:
                source = chosen.at[2 * step - 1 + direction if step else 0, along - 1]
            slot_copies[step].append(
                put(
                    source,
                    arrived.at[:, pl.ds(base + 2 * (NX - along), count)],
                    row_send.at[step, direction, along],
                    row_recv.at[step, direction, along],
                    rows_x[along],
                )
            )

    weight_copies, locals_weights, spread_copies = [], [], []

    def weights_along(turn):
        some = pl.ds(NZ // NX * turn, NZ // NX)
        for step in range(1, NX):
            weight_copies.append(
                put(
                    weight_column.at[some],
                    weights.at[core, NX - step, some],
                    weight_send.at[turn, step],
                    weight_recv.at[turn, step],
                    rows_x[step],
                )
            )
        locals_weights.append(local(weight_column.at[some], weights.at[core, 0, some], 3 + turn))

    def peer_weights():
        for copy in locals_weights:
            copy.wait()
        for copy in weight_copies:
            copy.wait_recv()
        spread_copies.append(put(weights.at[core], weights.at[core], peer_send, peer_recv, peer))

    def spread(source, target, number, send_sem, recv_sem, base, count):
        for step in range(1, HEADS):
            other = lax.rem(head + step, HEADS)
            spread_copies.append(
                put(
                    source.at[other, pl.ds(base, count)],
                    target.at[pl.ds(base, count), head],
                    send_sem.at[number, step],
                    recv_sem.at[number, step],
                    heads[step],
                )
            )
        copy = pltpu.make_async_copy(
            source.at[head, pl.ds(base, count)],
            target.at[pl.ds(base, count), head],
            send_sem.at[number, 0],
        )
        copy.start()
        locals_started.append(copy)

    lower_lanes = lax.broadcasted_iota(jnp.int32, (16 * PART, BLK), 1) < HD

    def store_tile(tile, target, other, base):
        count = tile.shape[0] // PART
        target[other, pl.ds(base, count)] = tile.astype(jnp.bfloat16).reshape(count, PART, BLK)

    def store_pairs(values_in, target, base):
        width_all = HEADS * HD
        keys = jnp.dot(
            values_in, qkv_weight[:, width_all : 2 * width_all], preferred_element_type=jnp.float32
        )
        values = jnp.dot(
            values_in, qkv_weight[:, 2 * width_all :], preferred_element_type=jnp.float32
        )
        is_lower = lower_lanes[: values_in.shape[0]]
        for pair in range(HEADS // 2):
            lanes = slice(pair * BLK, (pair + 1) * BLK)
            key, value = keys[:, lanes], values[:, lanes]
            even = jnp.where(is_lower, value, pltpu.roll(key, HD, 1))
            odd = jnp.where(is_lower, pltpu.roll(value, HD, 1), key)
            store_tile(even, target, 2 * pair, base)
            store_tile(odd, target, 2 * pair + 1, base)

    def store_queries(values_in, target, base):
        queries = jnp.dot(
            values_in, qkv_weight[:, : HEADS * HD], preferred_element_type=jnp.float32
        )
        queries = queries * (HD**-0.5)
        is_lower = lower_lanes[: values_in.shape[0]]
        for pair in range(HEADS // 2):
            query = queries[:, pair * BLK : (pair + 1) * BLK]
            store_tile(jnp.where(is_lower, 0.0, pltpu.roll(query, HD, 1)), target, 2 * pair, base)
            store_tile(jnp.where(is_lower, 0.0, query), target, 2 * pair + 1, base)

    def project_own():
        @pl.loop(0, 2)
        def _(step):
            blocks = pl.ds(16 * step, 16)
            joined = jnp.concatenate(
                [carried[part][blocks].reshape(16 * PART, part_width) for part in range(PARTS)], 1
            )
            store_queries(joined, sent_own.at[0], 16 * step)
            store_pairs(joined, sent_own.at[1], 16 * step)

        spread(sent_own.at[0], own_query, 0, own_send, own_recv, 0, 32)
        spread(sent_own.at[1], own_pair, 1, own_send, own_recv, 0, 32)

    def project(step):
        count = 16 if 0 < step < HALF_RING else 8
        base = slot_base(step)
        for copy in slot_copies[step]:
            copy.wait_recv()
        joined = jnp.concatenate(
            [
                arrived[part, pl.ds(base, count)].reshape(count * PART, part_width)
                for part in range(PARTS)
            ],
            1,
        )
        store_pairs(joined, sent_slot, base)
        spread(sent_slot, slot_pair, step, spread_send, spread_recv, base, count)

    ring, pools, table_z, handled = {}, [first_pool], [], set()

    def handle(hop, part):
        if (hop, part) in handled:
            return
        handled.add((hop, part))
        for direction in range(2):
            ring[direction, hop, part].wait_recv()
            if hop == FULL_HOPS:
                trim(direction, part)
            if hop < HALF_RING:
                ring_go(direction, hop + 1, part)
        if hop <= FULL_HOPS:
            for direction in range(2):
                slots_pick(hop, direction, part)

    def begin(part):
        for direction in range(2):
            ring_go(direction, 1, part)

    def during_first(moment):
        if moment == 0:
            pools.append(pool_own(1))
            own_row.wait()
            for copy in table_x:
                copy.wait_recv()
            plane_rows = tables.at[pl.ds(z * NX, NX)]
            for step in range(1, NZ):
                table_z.append(
                    put(
                        plane_rows,
                        plane_rows,
                        table_send.at[NX + step],
                        table_recv.at[NX + step],
                        planes[step],
                    )
                )
        if moment in (2, 5):
            weights_on({2: 1, 5: 2}[moment])

    def during_second(moment):
        if moment == 0:
            pools.append(pool_own(2))
        if moment in (1, 3, 5):
            weights_on({1: 3, 3: 4, 5: 5}[moment])
        if moment == 6:
            handle(1, 0)

    def during_third(moment):
        if moment in (1, 3, 5):
            weights_on({1: 6, 3: 7, 5: 8}[moment])
        if moment == 2:
            handle(2, 0)
        if moment == 6:
            handle(1, 1)

    gather_rows(0, pools[0], during_first)
    begin(0)
    for copy in table_z:
        copy.wait_recv()
    local(tables, wanted, 2).wait()
    slots_pick(0, 0, 0)
    gather_rows(1, pools[1], during_second)
    begin(1)
    slots_pick(0, 0, 1)
    gather_rows(2, pools[2], during_third)
    begin(2)
    slots_pick(0, 0, 2)
    slots_along(0, 0)
    own_weights.wait()

    for hop in range(1, HALF_RING + 1):
        for part in range(PARTS):
            handle(hop, part)
            if hop == 1 and part == 1:
                project_own()
        for direction in range(2):
            slots_along(hop, direction)
        if hop <= NX:
            weights_along(hop - 1)
        if hop == HALF_RING - 1:
            peer_weights()
        project(hop - 1)
    project(HALF_RING)
    for copy in spread_copies:
        copy.wait_recv()
    for copy in started:
        copy.wait_send()
    for copy in locals_started:
        copy.wait()


def exchange(features, picked, up_rows, down_rows, wanted_row, count_row, qkv_weight):
    rows, width = features.shape
    blocks, part_width = rows // PART, width // PARTS
    bf16 = jnp.bfloat16
    dma = pltpu.SemaphoreType.DMA
    tables = (NZ * NX, 1, 2 * wanted_row.shape[1])
    return pl.pallas_call(
        exchange_kernel,
        out_shape=(
            jax.ShapeDtypeStruct((blocks, HEADS, PART, BLK), bf16),
            jax.ShapeDtypeStruct((blocks, HEADS, PART, BLK), bf16),
            jax.ShapeDtypeStruct((2 * NZ * NX, HEADS, PART, BLK), bf16),
            jax.ShapeDtypeStruct((2, NX, NZ, 2, PART, width), bf16),
            jax.ShapeDtypeStruct(tables, jnp.int32),
        ),
        in_specs=[VMEM] * 7,
        out_specs=(ANY, ANY, ANY, ANY, ANY),
        scratch_shapes=[pltpu.VMEM((blocks, PART, part_width), bf16)]
        * ((2 * FULL_HOPS + 1) * PARTS)
        + [
            pltpu.VMEM((PARTS, 8, rows, part_width), bf16),
            pltpu.VMEM((rows, part_width), jnp.float32),
            pltpu.VMEM((2, PART, width), bf16),
            pltpu.VMEM((1,) + tables[1:], jnp.int32),
            pltpu.VMEM((NZ, 2, PART, width), bf16),
            pltpu.SMEM(tables, jnp.int32),
            pltpu.VMEM(
                (2, HALF_RING - FULL_HOPS, PARTS, hop_size(FULL_HOPS + 1), PART, part_width),
                bf16,
            ),
            pltpu.VMEM((2, PARTS, hop_size(FULL_HOPS + 1), PART, part_width), bf16),
            pltpu.VMEM((1 + 2 * FULL_HOPS, NX - 1, PARTS, 2, PART, part_width), bf16),
            pltpu.VMEM((PARTS, 2 * NZ * NX, PART, part_width), bf16),
            pltpu.VMEM((2, HEADS, blocks, PART, BLK), bf16),
            pltpu.VMEM((HEADS, 2 * NZ * NX, PART, BLK), bf16),
            dma((PARTS, 10)),
            dma((PARTS, 10)),
            dma((NX + NZ,)),
            dma((NX + NZ,)),
            dma((NZ,)),
            dma((NZ,)),
            dma((2, HALF_RING, PARTS)),
            dma((2, HALF_RING, PARTS)),
            dma((HALF_RING + 1, 2, NX)),
            dma((HALF_RING + 1, 2, NX)),
            dma((HALF_RING + 1, HEADS)),
            dma((HALF_RING + 1, HEADS)),
            dma((NX, NX)),
            dma((NX, NX)),
            dma((2, HEADS)),
            dma((2, HEADS)),
            dma,
            dma,
            dma((3 + NX,)),
        ],
        compiler_params=pltpu.CompilerParams(
            collective_id=1, has_side_effects=True, vmem_limit_bytes=LIMIT
        ),
        name="exchange_blocks",
    )(features, picked, up_rows, down_rows, wanted_row, count_row, qkv_weight)


def attend_kernel(
    dest, key_block, turn, row_count, tables, order, query, own_pair, slot_pair, out, held, *merged
):
    key_ids = lax.broadcasted_iota(jnp.int32, (BLK, BLK), 1)
    row_ids = lax.broadcasted_iota(jnp.int32, (BLK, BLK), 0)
    dom = lax.axis_index("dom")
    z, x = dom // NX, lax.rem(dom, NX)
    node_base = dom * order.shape[0]

    def slot_of(entry):
        owner = dest[entry]
        gap = lax.rem(z - owner // NX + NZ, NZ)
        start = jnp.where(gap <= HALF_RING, 16 * gap - 8, 16 * (NZ - gap))
        start = jnp.where(gap == 0, 0, start)
        across = lax.rem(lax.rem(owner, NX) - x + NX, NX)
        return start + 2 * across + turn[entry], tables[owner, 0, 2 * NZ * NX + key_block[entry]]

    def one(block, target):
        queries = query[block]
        first, first_count = slot_of(2 * block)
        second, second_count = slot_of(2 * block + 1)
        own_count = row_count[block]
        pairs = [own_pair[block], slot_pair[first], slot_pair[second]]
        scores = []
        for pair, count in zip(pairs, (own_count, first_count, second_count)):
            score = lax.dot_general(
                queries, pair, (((1,), (1,)), ((), ())), preferred_element_type=jnp.float32
            )
            scores.append(jnp.where(key_ids < count, score, -1e30))
        peak = jnp.max(jnp.maximum(jnp.maximum(scores[0], scores[1]), scores[2]), 1, keepdims=True)
        weights = [jnp.exp(score - peak) for score in scores]
        total = jnp.sum(weights[0] + weights[1] + weights[2], 1, keepdims=True)
        summed = sum(
            jnp.dot(weight.astype(jnp.bfloat16), pair, preferred_element_type=jnp.float32)
            for weight, pair in zip(weights, pairs)
        )
        target[...] = jnp.where(row_ids < own_count, summed / total, 0.0)

    def place(block, source):
        for piece in range(BLK // 8):
            values = source[pl.ds(8 * piece, 8)]
            for row in range(8):
                node = order[BLK * block + 8 * piece + row] - node_base
                held[pl.ds(node, 1), :] = values[row : row + 1, :]

    blocks = query.shape[0]

    @pl.loop(0, blocks // 4)
    def _(step):
        for side in range(2):
            pair = 2 * step + side
            before = lax.rem(pair + blocks // 2 - 1, blocks // 2)
            for number in range(2):
                one(2 * pair + number, merged[2 * side + number])
                place(2 * before + number, merged[2 * (1 - side) + number])

    for number in range(2):
        place(blocks - 2 + number, merged[2 + number])
    half = BLK * blocks // HEADS // 2
    is_lower = lax.broadcasted_iota(jnp.int32, (half, BLK), 1) < HD
    for owner in range(HEADS):
        first = held[pl.ds(2 * half * owner, half)]
        second = held[pl.ds(2 * half * owner + half, half)]
        out[owner] = jnp.where(is_lower, first, pltpu.roll(second, HD, 1)).astype(jnp.bfloat16)


def attend(dest, key_block, turn, row_count, tables, order, query, own_pair, slot_pair):
    rows = order.shape[0]
    return pl.pallas_call(
        attend_kernel,
        out_shape=jax.ShapeDtypeStruct((HEADS, rows // HEADS // 2, BLK), jnp.bfloat16),
        in_specs=[SMEM] * 6 + [VMEM] * 3,
        out_specs=VMEM,
        scratch_shapes=[pltpu.VMEM((rows, BLK), jnp.float32)]
        + [pltpu.VMEM((BLK, BLK), jnp.float32)] * 4,
        compiler_params=pltpu.CompilerParams(vmem_limit_bytes=LIMIT),
        name="attend_blocks",
    )(dest, key_block, turn, row_count, tables, order, query, own_pair, slot_pair)


def layer_norm(values, gain):
    centered = values - jnp.mean(values, -1, keepdims=True)
    spread = jnp.mean(centered * centered, -1, keepdims=True)
    return centered * lax.rsqrt(spread + 1e-05) * gain


def finish_kernel(
    features,
    attended,
    out_weight,
    attn_gain,
    weights,
    final_gain,
    out,
    grouped,
    spaced,
    units,
    mixed,
    send_sem,
    recv_sem,
    local_sem,
):
    head = lax.axis_index("head")
    others = [lax.rem(head + step, HEADS) for step in range(1, HEADS)]
    greet([{"head": other} for other in others])
    copies = [
        send(
            attended.at[other], grouped.at[head], send_sem.at[step], recv_sem.at[step], {"head": other}
        )
        for step, other in enumerate(others)
    ]
    own = pltpu.make_async_copy(attended.at[head], grouped.at[head], local_sem.at[0])
    own.start()
    load = pltpu.make_async_copy(weights, units, local_sem.at[1])
    load.start()
    gap = jnp.zeros((HD, out_weight.shape[1]), out_weight.dtype)
    for number in range(HEADS):
        block = out_weight[pl.ds(HD * number, HD)]
        for side in range(2):
            spaced[side, pl.ds(BLK * number + HD * side, HD)] = block
            spaced[side, pl.ds(BLK * number + HD * (1 - side), HD)] = gap
    own.wait()
    for copy in copies:
        copy.wait()
    joined = jnp.concatenate([grouped[number] for number in range(HEADS)], 1)
    half = joined.shape[0]
    for side in range(2):
        part = pl.ds(side * half, half)
        attention = jnp.dot(joined, spaced[side], preferred_element_type=jnp.float32)
        residual_sum = features[part].astype(jnp.float32) + attention
        mixed[part] = layer_norm(residual_sum, attn_gain[...])
    hidden_norm = mixed[...].astype(jnp.bfloat16)
    mixed[...] = hidden_norm.astype(jnp.float32)
    load.wait()
    tile = 512
    for step in range(units.shape[1] // tile):
        here = pl.ds(step * tile, tile)
        hidden = lax.dot_general(
            hidden_norm,
            units[0, here],
            (((1,), (1,)), ((), ())),
            preferred_element_type=jnp.float32,
        )
        hidden = jax.nn.gelu(hidden).astype(jnp.bfloat16)
        mixed[...] += jnp.dot(hidden, units[1, here], preferred_element_type=jnp.float32)
    out[...] = layer_norm(mixed[...], final_gain[...]).astype(jnp.bfloat16)


def finish(features, attended, out_weight, attn_gain, weights, final_gain):
    dma = pltpu.SemaphoreType.DMA
    return pl.pallas_call(
        finish_kernel,
        out_shape=jax.ShapeDtypeStruct(features.shape, jnp.bfloat16),
        in_specs=[VMEM] * 4 + [ANY, VMEM],
        out_specs=VMEM,
        scratch_shapes=[
            pltpu.VMEM(attended.shape, jnp.bfloat16),
            pltpu.VMEM((2, HEADS * BLK, features.shape[1]), jnp.bfloat16),
            pltpu.VMEM(weights.shape, jnp.bfloat16),
            pltpu.VMEM(features.shape, jnp.float32),
            dma((HEADS - 1,)),
            dma((HEADS - 1,)),
            dma((2,)),
        ],
        compiler_params=pltpu.CompilerParams(
            collective_id=2, has_side_effects=True, vmem_limit_bytes=LIMIT
        ),
        name="finish_rows",
    )(features, attended, out_weight, attn_gain, weights, final_gain)


def per_device(
    features,
    qkv_weight,
    out_weight,
    attn_gain,
    up_weight,
    down_weight,
    final_gain,
    node_order,
    dest_part,
    key_block,
    row_count,
):
    blocks = dest_part.shape[0]
    partitions = NZ * NX
    width = features.shape[1]
    dom, head = lax.axis_index("dom"), lax.axis_index("head")

    dest_flat, block_flat = dest_part.reshape(-1), key_block.reshape(-1)
    earlier = jnp.tril(dest_flat[:, None] == dest_flat[None, :], -1)
    turn = jnp.sum(earlier.astype(jnp.int32), 1)
    entry = (2 * dest_flat + turn)[:, None] == jnp.arange(2 * partitions, dtype=jnp.int32)[None, :]
    wanted = jnp.sum(jnp.where(entry, block_flat[:, None], 0), 0, keepdims=True)

    picked = lax.dynamic_index_in_dim(
        node_order.reshape(blocks, HEADS, PART), head, 1, keepdims=False
    ).reshape(-1, 1)
    picked = picked - dom * node_order.shape[0]
    own_query, own_pair, slot_pair, weights, tables = exchange(
        features,
        picked,
        up_weight.T,
        down_weight,
        wanted,
        row_count.reshape(1, -1),
        qkv_weight,
    )
    attended = attend(
        dest_flat,
        block_flat,
        turn,
        row_count,
        tables,
        node_order,
        own_query.reshape(blocks, BLK, BLK),
        own_pair.reshape(blocks, BLK, BLK),
        slot_pair.reshape(2 * partitions, BLK, BLK),
    )
    return finish(
        features,
        attended,
        out_weight,
        attn_gain.reshape(1, width),
        weights.reshape(2, partitions * 2 * PART, width),
        final_gain.reshape(1, width),
    )


def solution(mesh):
    in_specs = (
        P(("dom", "head"), None),
        P(),
        P(),
        P(),
        P(None, "dom"),
        P("dom", None),
        P(),
        P("dom"),
        P("dom", None),
        P("dom", None),
        P("dom"),
    )
    out_specs = P(("dom", "head"), None)
    return jax.shard_map(
        per_device, mesh=mesh, in_specs=in_specs, out_specs=out_specs, check_vma=False
    )
```

```python
import functools

import jax
import jax.numpy as jnp
from jax import lax
from jax.experimental import pallas as pl
from jax.experimental.pallas import tpu as pltpu
from jax.sharding import PartitionSpec as P

HEADS = 8
HD = 64
BLK = 128
NZ = 16
NX = 4
PART = BLK // HEADS
HALF_RING = NZ // 2
FULL_HOPS = 4
PARTS = 3
MESH = pl.DeviceIdType.MESH
VMEM = pl.BlockSpec(memory_space=pltpu.VMEM)
SMEM = pl.BlockSpec(memory_space=pltpu.SMEM)
ANY = pl.BlockSpec(memory_space=pl.ANY)
LIMIT = 60 * 1024 * 1024


def greet(partners):
    barrier = pltpu.get_barrier_semaphore()
    for partner in partners:
        pl.semaphore_signal(barrier, inc=1, device_id=partner, device_id_type=MESH)
    pl.semaphore_wait(barrier, len(partners))


def send(source, target, send_sem, recv_sem, partner):
    copy = pltpu.make_async_remote_copy(
        src_ref=source,
        dst_ref=target,
        send_sem=send_sem,
        recv_sem=recv_sem,
        device_id=partner,
        device_id_type=MESH,
    )
    copy.start()
    return copy


def hop_size(hop):
    return 32 if hop <= FULL_HOPS else 4 + 8 * (HALF_RING - hop)


def slot_base(step):
    return 0 if step == 0 else 8 + 16 * (step - 1)


def exchange_kernel(*refs):
    inputs, outputs, scratch = refs[:7], refs[7:12], refs[12:]
    whole = (2 * FULL_HOPS + 1) * PARTS
    exchange_body(*inputs, *outputs, scratch[:PARTS], scratch[PARTS:whole], *scratch[whole:])


def exchange_body(
    features,
    picked,
    up_rows,
    down_rows,
    wanted_row,
    count_row,
    qkv_weight,
    own_query,
    own_pair,
    slot_pair,
    weights,
    tables,
    carried,
    full,
    pool,
    total,
    extra,
    own_table,
    weight_column,
    wanted,
    part_way,
    trimmed,
    chosen,
    arrived,
    sent_own,
    sent_slot,
    pool_send,
    pool_recv,
    table_send,
    table_recv,
    column_send,
    column_recv,
    ring_send,
    ring_recv,
    row_send,
    row_recv,
    spread_send,
    spread_recv,
    weight_send,
    weight_recv,
    own_send,
    own_recv,
    peer_send,
    peer_recv,
    local_sem,
):
    dom, head = lax.axis_index("dom"), lax.axis_index("head")
    z, x = dom // NX, lax.rem(dom, NX)
    y, core = head // 2, lax.rem(head, 2)
    rows, width = features.shape
    part_width = width // PARTS

    def plane(step):
        return lax.rem(z + step + NZ, NZ)

    def column(step):
        return lax.rem(x + step, NX)

    def at(step, other):
        return lax.rem(y + step, 4) * 2 + lax.rem(core + other, 2)

    planes = [None] + [{"dom": plane(step) * NX + x} for step in range(1, NZ)]
    rows_x = [None] + [{"dom": z * NX + column(step)} for step in range(1, NX)]
    heads = [None] + [{"head": lax.rem(head + step, HEADS)} for step in range(1, HEADS)]
    right, left, peer = {"head": at(1, 0)}, {"head": at(3, 0)}, {"head": at(0, 1)}
    up, down = planes[1], planes[NZ - 1]
    greet(planes[1:] + rows_x[1:] + heads[1:])
    started, locals_started = [], []

    def put(*operands):
        started.append(send(*operands))
        return started[-1]

    def local(source, target, number):
        copy = pltpu.make_async_copy(source, target, local_sem.at[number])
        copy.start()
        return copy

    half = rows // 2
    upper, lower = pl.ds(0, half), pl.ds(half, half)

    def pool_go(part, number, source, slot, which, partner):
        target = pool.at[part, slot] if which is None else pool.at[part, slot, which]
        return put(source, target, pool_send.at[part, number], pool_recv.at[part, number], partner)

    def pool_own(part):
        lanes = pl.ds(part * part_width, part_width)
        return {
            "right_a": pool_go(part, 0, features.at[upper, lanes], 1, upper, right),
            "left_b": pool_go(part, 1, features.at[lower, lanes], 2, lower, left),
            "right_b": pool_go(part, 2, features.at[lower, lanes], 1, lower, right),
            "left_a": pool_go(part, 3, features.at[upper, lanes], 2, upper, left),
            "own_peer": pool_go(part, 4, features.at[:, lanes], 4, None, peer),
        }

    def weights_go(direction, hop):
        place = HALF_RING * direction + hop
        return put(
            extra if hop == 1 else weight_column.at[place - 1],
            weight_column.at[place],
            column_send.at[place],
            column_recv.at[place],
            up if direction == 0 else down,
        )

    first_pool = pool_own(0)
    own_table[0, :, : wanted_row.shape[1]] = wanted_row[...]
    own_table[0, :, wanted_row.shape[1] :] = jnp.zeros_like(wanted_row)
    own_table[0, :, pl.ds(wanted_row.shape[1], count_row.shape[1])] = count_row[...]
    table_x = [
        put(own_table, tables.at[pl.ds(dom, 1)], table_send.at[step], table_recv.at[step], rows_x[step])
        for step in range(1, NX)
    ]
    own_row = local(own_table, tables.at[pl.ds(dom, 1)], 0)
    units = jnp.where(core == 0, up_rows[...], down_rows[...])
    filler = jnp.zeros((2 * PART - units.shape[0], width), units.dtype)
    extra[...] = jnp.concatenate([units, filler], 0).reshape(2, PART, width)
    hops = [weights_go(0, 1), weights_go(1, 1)]
    own_weights = local(extra, weight_column.at[0], 1)

    def weights_on(hop):
        for direction in range(2):
            if hops[direction] is not None:
                hops[direction].wait_recv()
                last = hop == HALF_RING - direction
                hops[direction] = None if last else weights_go(direction, hop + 1)

    row_ids = lax.broadcasted_iota(jnp.int32, (rows, rows), 1)
    picks = picked[...]

    def add(block, owner, first=False):
        hit = jnp.where(picks - owner * rows == row_ids, 1.0, 0.0).astype(jnp.bfloat16)
        product = jnp.dot(hit, block, preferred_element_type=jnp.float32)
        total[...] = product if first else total[...] + product

    def gather_rows(part, got, along):
        add(features[:, part * part_width : (part + 1) * part_width], head, True)
        got["right_a"].wait_recv()
        on_a = pool_go(part, 5, pool.at[part, 1, upper], 3, upper, right)
        got["left_b"].wait_recv()
        on_b = pool_go(part, 6, pool.at[part, 2, lower], 3, lower, left)
        along(0)
        got["own_peer"].wait_recv()
        add(pool[part, 4], at(0, 1))
        along(1)
        got["right_b"].wait_recv()
        from_left = pool_go(part, 7, pool.at[part, 1], 5, None, peer)
        got["left_a"].wait_recv()
        from_right = pool_go(part, 8, pool.at[part, 2], 6, None, peer)
        along(2)
        add(pool[part, 1], at(3, 0))
        along(3)
        add(pool[part, 2], at(1, 0))
        along(4)
        from_left.wait_recv()
        add(pool[part, 5], at(3, 1))
        along(5)
        from_right.wait_recv()
        add(pool[part, 6], at(1, 1))
        along(6)
        on_a.wait_recv()
        on_b.wait_recv()
        across = pool_go(part, 9, pool.at[part, 3], 7, None, peer)
        add(pool[part, 3], at(2, 0))
        along(7)
        across.wait_recv()
        add(pool[part, 7], at(2, 1))
        carried[part][...] = (
            total[...].astype(jnp.bfloat16).reshape(rows // PART, PART, part_width)
        )

    def landing(direction, hop, part):
        if hop <= FULL_HOPS:
            return full[PARTS * (2 * (hop - 1) + direction) + part]
        return part_way.at[direction, hop - FULL_HOPS - 1, part]

    def ring_go(direction, hop, part):
        if hop == 1:
            source = carried[part]
        elif hop == FULL_HOPS + 1:
            source = trimmed.at[direction, part]
        else:
            source = landing(direction, hop - 1, part)
        count = pl.ds(0, hop_size(hop))
        ring[direction, hop, part] = put(
            source.at[count],
            landing(direction, hop, part).at[count],
            ring_send.at[direction, hop - 1, part],
            ring_recv.at[direction, hop - 1, part],
            up if direction == 0 else down,
        )

    def listed(plane_step, column_id, source, turn):
        return wanted[plane(plane_step) * NX + column_id, 0, 2 * source + turn]

    def trim(direction, part):
        chunk = landing(direction, FULL_HOPS, part)
        sign = 1 if direction == 0 else -1
        source = plane(-sign * FULL_HOPS) * NX + x
        beyond = HALF_RING - FULL_HOPS
        for column_id in range(NX):
            trimmed[direction, part, column_id] = chunk[
                listed(sign * beyond, column_id, source, direction)
            ]
        for ahead in range(beyond - 1, 0, -1):
            first = 4 + 8 * (beyond - 1 - ahead)
            for column_id in range(NX):
                for turn in range(2):
                    trimmed[direction, part, first + 2 * column_id + turn] = chunk[
                        listed(sign * ahead, column_id, source, turn)
                    ]

    slot_copies = {step: [] for step in range(HALF_RING + 1)}

    def slots_pick(step, direction, part):
        base = slot_base(step) + 8 * direction
        chunk = landing(direction, step, part) if step else carried[part]
        source = plane(-step if direction == 0 else step) * NX + x
        buffer = 2 * step - 1 + direction if step else 0
        for turn in range(2):
            arrived[part, base + turn] = chunk[listed(0, x, source, turn)]
        for along in range(1, NX):
            for turn in range(2):
                chosen[buffer, along - 1, part, turn] = chunk[
                    listed(0, column(along), source, turn)
                ]

    def slots_along(step, direction):
        count, base = 2, slot_base(step) + 8 * direction
        if step > FULL_HOPS:
            chunk = part_way.at[direction, step - FULL_HOPS - 1]
            first = 4 + 8 * (HALF_RING - 1 - step)
            if step == HALF_RING:
                first, count, base = 0, 1, slot_base(step) + direction
            arrived[:, pl.ds(base, count)] = chunk[:, pl.ds(first + count * x, count)]
        for along in range(1, NX):
            if step > FULL_HOPS:
                source = chunk.at[:, pl.ds(first + count * column(along), count)]
            else:
                source = chosen.at[2 * step - 1 + direction if step else 0, along - 1]
            slot_copies[step].append(
                put(
                    source,
                    arrived.at[:, pl.ds(base + 2 * (NX - along), count)],
                    row_send.at[step, direction, along],
                    row_recv.at[step, direction, along],
                    rows_x[along],
                )
            )

    weight_copies, locals_weights, spread_copies = [], [], []

    def weights_along(turn):
        some = pl.ds(NZ // NX * turn, NZ // NX)
        for step in range(1, NX):
            weight_copies.append(
                put(
                    weight_column.at[some],
                    weights.at[core, NX - step, some],
                    weight_send.at[turn, step],
                    weight_recv.at[turn, step],
                    rows_x[step],
                )
            )
        locals_weights.append(local(weight_column.at[some], weights.at[core, 0, some], 3 + turn))

    def peer_weights():
        for copy in locals_weights:
            copy.wait()
        for copy in weight_copies:
            copy.wait_recv()
        spread_copies.append(put(weights.at[core], weights.at[core], peer_send, peer_recv, peer))

    def spread(source, target, number, send_sem, recv_sem, base, count):
        for step in range(1, HEADS):
            other = lax.rem(head + step, HEADS)
            spread_copies.append(
                put(
                    source.at[other, pl.ds(base, count)],
                    target.at[pl.ds(base, count), head],
                    send_sem.at[number, step],
                    recv_sem.at[number, step],
                    heads[step],
                )
            )
        copy = pltpu.make_async_copy(
            source.at[head, pl.ds(base, count)],
            target.at[pl.ds(base, count), head],
            send_sem.at[number, 0],
        )
        copy.start()
        locals_started.append(copy)

    lower_lanes = lax.broadcasted_iota(jnp.int32, (16 * PART, BLK), 1) < HD

    def store_tile(tile, target, other, base):
        count = tile.shape[0] // PART
        target[other, pl.ds(base, count)] = tile.astype(jnp.bfloat16).reshape(count, PART, BLK)

    def store_pairs(values_in, target, base):
        width_all = HEADS * HD
        keys = jnp.dot(
            values_in, qkv_weight[:, width_all : 2 * width_all], preferred_element_type=jnp.float32
        )
        values = jnp.dot(
            values_in, qkv_weight[:, 2 * width_all :], preferred_element_type=jnp.float32
        )
        is_lower = lower_lanes[: values_in.shape[0]]
        for pair in range(HEADS // 2):
            lanes = slice(pair * BLK, (pair + 1) * BLK)
            key, value = keys[:, lanes], values[:, lanes]
            even = jnp.where(is_lower, value, pltpu.roll(key, HD, 1))
            odd = jnp.where(is_lower, pltpu.roll(value, HD, 1), key)
            store_tile(even, target, 2 * pair, base)
            store_tile(odd, target, 2 * pair + 1, base)

    def store_queries(values_in, target, base):
        queries = jnp.dot(
            values_in, qkv_weight[:, : HEADS * HD], preferred_element_type=jnp.float32
        )
        queries = queries * (HD**-0.5)
        is_lower = lower_lanes[: values_in.shape[0]]
        for pair in range(HEADS // 2):
            query = queries[:, pair * BLK : (pair + 1) * BLK]
            store_tile(jnp.where(is_lower, 0.0, pltpu.roll(query, HD, 1)), target, 2 * pair, base)
            store_tile(jnp.where(is_lower, 0.0, query), target, 2 * pair + 1, base)

    def project_own():
        @pl.loop(0, 2)
        def _(step):
            blocks = pl.ds(16 * step, 16)
            joined = jnp.concatenate(
                [carried[part][blocks].reshape(16 * PART, part_width) for part in range(PARTS)], 1
            )
            store_queries(joined, sent_own.at[0], 16 * step)
            store_pairs(joined, sent_own.at[1], 16 * step)

        spread(sent_own.at[0], own_query, 0, own_send, own_recv, 0, 32)
        spread(sent_own.at[1], own_pair, 1, own_send, own_recv, 0, 32)

    def project(step):
        count = 16 if 0 < step < HALF_RING else 8
        base = slot_base(step)
        for copy in slot_copies[step]:
            copy.wait_recv()
        joined = jnp.concatenate(
            [
                arrived[part, pl.ds(base, count)].reshape(count * PART, part_width)
                for part in range(PARTS)
            ],
            1,
        )
        store_pairs(joined, sent_slot, base)
        spread(sent_slot, slot_pair, step, spread_send, spread_recv, base, count)

    ring, pools, table_z, handled = {}, [first_pool], [], set()

    def handle(hop, part):
        if (hop, part) in handled:
            return
        handled.add((hop, part))
        for direction in range(2):
            ring[direction, hop, part].wait_recv()
            if hop == FULL_HOPS:
                trim(direction, part)
            if hop < HALF_RING:
                ring_go(direction, hop + 1, part)
        if hop <= FULL_HOPS:
            for direction in range(2):
                slots_pick(hop, direction, part)

    def begin(part):
        for direction in range(2):
            ring_go(direction, 1, part)

    def during_first(moment):
        if moment == 0:
            pools.append(pool_own(1))
            own_row.wait()
            for copy in table_x:
                copy.wait_recv()
            plane_rows = tables.at[pl.ds(z * NX, NX)]
            for step in range(1, NZ):
                table_z.append(
                    put(
                        plane_rows,
                        plane_rows,
                        table_send.at[NX + step],
                        table_recv.at[NX + step],
                        planes[step],
                    )
                )
        if moment in (2, 5):
            weights_on({2: 1, 5: 2}[moment])

    def during_second(moment):
        if moment == 0:
            pools.append(pool_own(2))
        if moment in (1, 3, 5):
            weights_on({1: 3, 3: 4, 5: 5}[moment])
        if moment == 6:
            handle(1, 0)

    def during_third(moment):
        if moment in (1, 3, 5):
            weights_on({1: 6, 3: 7, 5: 8}[moment])
        if moment == 2:
            handle(2, 0)
        if moment == 6:
            handle(1, 1)

    gather_rows(0, pools[0], during_first)
    begin(0)
    for copy in table_z:
        copy.wait_recv()
    local(tables, wanted, 2).wait()
    slots_pick(0, 0, 0)
    gather_rows(1, pools[1], during_second)
    begin(1)
    slots_pick(0, 0, 1)
    gather_rows(2, pools[2], during_third)
    begin(2)
    slots_pick(0, 0, 2)
    slots_along(0, 0)
    own_weights.wait()

    for hop in range(1, HALF_RING + 1):
        for part in range(PARTS):
            handle(hop, part)
            if hop == 1 and part == 1:
                project_own()
        for direction in range(2):
            slots_along(hop, direction)
        if hop <= NX:
            weights_along(hop - 1)
        if hop == HALF_RING - 2:
            peer_weights()
        project(hop - 1)
    project(HALF_RING)
    for copy in spread_copies:
        copy.wait_recv()
    for copy in started:
        copy.wait_send()
    for copy in locals_started:
        copy.wait()


def exchange(features, picked, up_rows, down_rows, wanted_row, count_row, qkv_weight):
    rows, width = features.shape
    blocks, part_width = rows // PART, width // PARTS
    bf16 = jnp.bfloat16
    dma = pltpu.SemaphoreType.DMA
    tables = (NZ * NX, 1, 2 * wanted_row.shape[1])
    return pl.pallas_call(
        exchange_kernel,
        out_shape=(
            jax.ShapeDtypeStruct((blocks, HEADS, PART, BLK), bf16),
            jax.ShapeDtypeStruct((blocks, HEADS, PART, BLK), bf16),
            jax.ShapeDtypeStruct((2 * NZ * NX, HEADS, PART, BLK), bf16),
            jax.ShapeDtypeStruct((2, NX, NZ, 2, PART, width), bf16),
            jax.ShapeDtypeStruct(tables, jnp.int32),
        ),
        in_specs=[VMEM] * 7,
        out_specs=(ANY, ANY, ANY, ANY, ANY),
        scratch_shapes=[pltpu.VMEM((blocks, PART, part_width), bf16)]
        * ((2 * FULL_HOPS + 1) * PARTS)
        + [
            pltpu.VMEM((PARTS, 8, rows, part_width), bf16),
            pltpu.VMEM((rows, part_width), jnp.float32),
            pltpu.VMEM((2, PART, width), bf16),
            pltpu.VMEM((1,) + tables[1:], jnp.int32),
            pltpu.VMEM((NZ, 2, PART, width), bf16),
            pltpu.SMEM(tables, jnp.int32),
            pltpu.VMEM(
                (2, HALF_RING - FULL_HOPS, PARTS, hop_size(FULL_HOPS + 1), PART, part_width),
                bf16,
            ),
            pltpu.VMEM((2, PARTS, hop_size(FULL_HOPS + 1), PART, part_width), bf16),
            pltpu.VMEM((1 + 2 * FULL_HOPS, NX - 1, PARTS, 2, PART, part_width), bf16),
            pltpu.VMEM((PARTS, 2 * NZ * NX, PART, part_width), bf16),
            pltpu.VMEM((2, HEADS, blocks, PART, BLK), bf16),
            pltpu.VMEM((HEADS, 2 * NZ * NX, PART, BLK), bf16),
            dma((PARTS, 10)),
            dma((PARTS, 10)),
            dma((NX + NZ,)),
            dma((NX + NZ,)),
            dma((NZ,)),
            dma((NZ,)),
            dma((2, HALF_RING, PARTS)),
            dma((2, HALF_RING, PARTS)),
            dma((HALF_RING + 1, 2, NX)),
            dma((HALF_RING + 1, 2, NX)),
            dma((HALF_RING + 1, HEADS)),
            dma((HALF_RING + 1, HEADS)),
            dma((NX, NX)),
            dma((NX, NX)),
            dma((2, HEADS)),
            dma((2, HEADS)),
            dma,
            dma,
            dma((3 + NX,)),
        ],
        compiler_params=pltpu.CompilerParams(
            collective_id=1, has_side_effects=True, vmem_limit_bytes=LIMIT
        ),
        name="exchange_blocks",
    )(features, picked, up_rows, down_rows, wanted_row, count_row, qkv_weight)


def attend_kernel(
    dest, key_block, turn, row_count, tables, order, query, own_pair, slot_pair, out, held, *merged
):
    key_ids = lax.broadcasted_iota(jnp.int32, (BLK, BLK), 1)
    row_ids = lax.broadcasted_iota(jnp.int32, (BLK, BLK), 0)
    dom = lax.axis_index("dom")
    z, x = dom // NX, lax.rem(dom, NX)
    node_base = dom * order.shape[0]

    def slot_of(entry):
        owner = dest[entry]
        gap = lax.rem(z - owner // NX + NZ, NZ)
        start = jnp.where(gap <= HALF_RING, 16 * gap - 8, 16 * (NZ - gap))
        start = jnp.where(gap == 0, 0, start)
        across = lax.rem(lax.rem(owner, NX) - x + NX, NX)
        return start + 2 * across + turn[entry], tables[owner, 0, 2 * NZ * NX + key_block[entry]]

    def one(block, target):
        queries = query[block]
        first, first_count = slot_of(2 * block)
        second, second_count = slot_of(2 * block + 1)
        own_count = row_count[block]
        pairs = [own_pair[block], slot_pair[first], slot_pair[second]]
        scores = []
        for pair, count in zip(pairs, (own_count, first_count, second_count)):
            score = lax.dot_general(
                queries, pair, (((1,), (1,)), ((), ())), preferred_element_type=jnp.float32
            )
            scores.append(jnp.where(key_ids < count, score, -1e30))
        peak = jnp.max(jnp.maximum(jnp.maximum(scores[0], scores[1]), scores[2]), 1, keepdims=True)
        weights = [jnp.exp(score - peak) for score in scores]
        total = jnp.sum(weights[0] + weights[1] + weights[2], 1, keepdims=True)
        summed = sum(
            jnp.dot(weight.astype(jnp.bfloat16), pair, preferred_element_type=jnp.float32)
            for weight, pair in zip(weights, pairs)
        )
        target[...] = jnp.where(row_ids < own_count, summed / total, 0.0)

    def place(block, source):
        for piece in range(BLK // 8):
            values = source[pl.ds(8 * piece, 8)]
            for row in range(8):
                node = order[BLK * block + 8 * piece + row] - node_base
                held[pl.ds(node, 1), :] = values[row : row + 1, :]

    blocks = query.shape[0]

    @pl.loop(0, blocks // 4)
    def _(step):
        for side in range(2):
            pair = 2 * step + side
            before = lax.rem(pair + blocks // 2 - 1, blocks // 2)
            for number in range(2):
                one(2 * pair + number, merged[2 * side + number])
                place(2 * before + number, merged[2 * (1 - side) + number])

    for number in range(2):
        place(blocks - 2 + number, merged[2 + number])
    half = BLK * blocks // HEADS // 2
    is_lower = lax.broadcasted_iota(jnp.int32, (half, BLK), 1) < HD
    for owner in range(HEADS):
        first = held[pl.ds(2 * half * owner, half)]
        second = held[pl.ds(2 * half * owner + half, half)]
        out[owner] = jnp.where(is_lower, first, pltpu.roll(second, HD, 1)).astype(jnp.bfloat16)


def attend(dest, key_block, turn, row_count, tables, order, query, own_pair, slot_pair):
    rows = order.shape[0]
    return pl.pallas_call(
        attend_kernel,
        out_shape=jax.ShapeDtypeStruct((HEADS, rows // HEADS // 2, BLK), jnp.bfloat16),
        in_specs=[SMEM] * 6 + [VMEM] * 3,
        out_specs=VMEM,
        scratch_shapes=[pltpu.VMEM((rows, BLK), jnp.float32)]
        + [pltpu.VMEM((BLK, BLK), jnp.float32)] * 4,
        compiler_params=pltpu.CompilerParams(vmem_limit_bytes=LIMIT),
        name="attend_blocks",
    )(dest, key_block, turn, row_count, tables, order, query, own_pair, slot_pair)


def layer_norm(values, gain):
    centered = values - jnp.mean(values, -1, keepdims=True)
    spread = jnp.mean(centered * centered, -1, keepdims=True)
    return centered * lax.rsqrt(spread + 1e-05) * gain


def finish_kernel(
    features,
    attended,
    out_weight,
    attn_gain,
    weights,
    final_gain,
    out,
    grouped,
    spaced,
    units,
    mixed,
    send_sem,
    recv_sem,
    local_sem,
):
    head = lax.axis_index("head")
    others = [lax.rem(head + step, HEADS) for step in range(1, HEADS)]
    greet([{"head": other} for other in others])
    copies = [
        send(
            attended.at[other], grouped.at[head], send_sem.at[step], recv_sem.at[step], {"head": other}
        )
        for step, other in enumerate(others)
    ]
    own = pltpu.make_async_copy(attended.at[head], grouped.at[head], local_sem.at[0])
    own.start()
    load = pltpu.make_async_copy(weights, units, local_sem.at[1])
    load.start()
    gap = jnp.zeros((HD, out_weight.shape[1]), out_weight.dtype)
    for number in range(HEADS):
        block = out_weight[pl.ds(HD * number, HD)]
        for side in range(2):
            spaced[side, pl.ds(BLK * number + HD * side, HD)] = block
            spaced[side, pl.ds(BLK * number + HD * (1 - side), HD)] = gap
    own.wait()
    for copy in copies:
        copy.wait()
    joined = jnp.concatenate([grouped[number] for number in range(HEADS)], 1)
    half = joined.shape[0]
    for side in range(2):
        part = pl.ds(side * half, half)
        attention = jnp.dot(joined, spaced[side], preferred_element_type=jnp.float32)
        residual_sum = features[part].astype(jnp.float32) + attention
        mixed[part] = layer_norm(residual_sum, attn_gain[...].reshape(1, -1))
    hidden_norm = mixed[...].astype(jnp.bfloat16)
    mixed[...] = hidden_norm.astype(jnp.float32)
    load.wait()
    tile = 512
    for step in range(units.shape[1] // tile):
        here = pl.ds(step * tile, tile)
        hidden = lax.dot_general(
            hidden_norm,
            units[0, here],
            (((1,), (1,)), ((), ())),
            preferred_element_type=jnp.float32,
        )
        hidden = jax.nn.gelu(hidden).astype(jnp.bfloat16)
        mixed[...] += jnp.dot(hidden, units[1, here], preferred_element_type=jnp.float32)
    out[...] = layer_norm(mixed[...], final_gain[...].reshape(1, -1)).astype(jnp.bfloat16)


def finish(features, attended, out_weight, attn_gain, weights, final_gain):
    dma = pltpu.SemaphoreType.DMA
    return pl.pallas_call(
        finish_kernel,
        out_shape=jax.ShapeDtypeStruct(features.shape, jnp.bfloat16),
        in_specs=[VMEM] * 4 + [ANY, VMEM],
        out_specs=VMEM,
        scratch_shapes=[
            pltpu.VMEM(attended.shape, jnp.bfloat16),
            pltpu.VMEM((2, HEADS * BLK, features.shape[1]), jnp.bfloat16),
            pltpu.VMEM(weights.shape, jnp.bfloat16),
            pltpu.VMEM(features.shape, jnp.float32),
            dma((HEADS - 1,)),
            dma((HEADS - 1,)),
            dma((2,)),
        ],
        compiler_params=pltpu.CompilerParams(
            collective_id=2, has_side_effects=True, vmem_limit_bytes=LIMIT
        ),
        name="finish_rows",
    )(features, attended, out_weight, attn_gain, weights, final_gain)


def per_device(
    features,
    qkv_weight,
    out_weight,
    attn_gain,
    up_weight,
    down_weight,
    final_gain,
    node_order,
    dest_part,
    key_block,
    row_count,
):
    blocks = dest_part.shape[0]
    partitions = NZ * NX
    width = features.shape[1]
    dom, head = lax.axis_index("dom"), lax.axis_index("head")

    dest_flat, block_flat = dest_part.reshape(-1), key_block.reshape(-1)
    earlier = jnp.tril(dest_flat[:, None] == dest_flat[None, :], -1)
    turn = jnp.sum(earlier.astype(jnp.int32), 1)
    entry = (2 * dest_flat + turn)[:, None] == jnp.arange(2 * partitions, dtype=jnp.int32)[None, :]
    wanted = jnp.sum(jnp.where(entry, block_flat[:, None], 0), 0, keepdims=True)

    picked = lax.dynamic_index_in_dim(
        node_order.reshape(blocks, HEADS, PART), head, 1, keepdims=False
    ).reshape(-1, 1)
    picked = picked - dom * node_order.shape[0]
    own_query, own_pair, slot_pair, weights, tables = exchange(
        features,
        picked,
        up_weight.T,
        down_weight,
        wanted,
        row_count.reshape(1, -1),
        qkv_weight,
    )
    attended = attend(
        dest_flat,
        block_flat,
        turn,
        row_count,
        tables,
        node_order,
        own_query.reshape(blocks, BLK, BLK),
        own_pair.reshape(blocks, BLK, BLK),
        slot_pair.reshape(2 * partitions, BLK, BLK),
    )
    return finish(
        features,
        attended,
        out_weight,
        attn_gain,
        weights.reshape(2, partitions * 2 * PART, width),
        final_gain,
    )


def solution(mesh):
    in_specs = (
        P(("dom", "head"), None),
        P(),
        P(),
        P(),
        P(None, "dom"),
        P("dom", None),
        P(),
        P("dom"),
        P("dom", None),
        P("dom", None),
        P("dom"),
    )
    out_specs = P(("dom", "head"), None)
    return jax.shard_map(
        per_device, mesh=mesh, in_specs=in_specs, out_specs=out_specs, check_vma=False
    )
```
